32 devices in a mesh: section: 2 (over x), tensor: 4 (over z), dp: 4 (over y, core).
Axes of the slice: x: 2, y: 2, z: 4, core: 2. Of those that a mesh axis runs over, the one named last changes fastest.
Arguments:
- hidden_in: bfloat16 [2, 4, 1024, 1024], P(None, 'dp', 'tensor'), may hold values from -6 to 6
- cotangent: bfloat16 [2, 4, 1024, 1024], P(None, 'dp', 'tensor'), may hold values from -6 to 6
- query_w: bfloat16 [2, 1024, 1024], P('section', None, 'tensor'), may hold values from -0.1875 to 0.1875
- key_w: bfloat16 [2, 1024, 1024], P('section', None, 'tensor'), may hold values from -0.1875 to 0.1875
- value_w: bfloat16 [2, 1024, 1024], P('section', None, 'tensor'), may hold values from -0.1875 to 0.1875
- output_w: bfloat16 [2, 1024, 1024], P('section', 'tensor'), may hold values from -0.1875 to 0.1875
- qk_scale: float32 [2, 1024], P('section', 'tensor'), may hold values from 0.25 to 1.75
- attn_rate: float32 [2, 1024], P('section'), may hold values from 0.1 to 0.6
- up_w: bfloat16 [2, 1024, 4096], P('section', None, 'tensor'), may hold values from -0.1875 to 0.1875
- gate_w: bfloat16 [2, 1024, 4096], P('section', None, 'tensor'), may hold values from -0.1875 to 0.1875
- down_w: bfloat16 [2, 4096, 1024], P('section', 'tensor'), may hold values from -0.09375 to 0.09375
- up_scale: float32 [2, 4096], P('section', 'tensor'), may hold values from 0.25 to 1.75
- gate_scale: float32 [2, 4096], P('section', 'tensor'), may hold values from 0.25 to 1.75
- mlp_rate: float32 [2, 1024], P('section'), may hold values from 0.1 to 0.6
Outputs:
- hidden_out: bfloat16 [2, 2, 4, 1024, 1024], P('section', None, 'dp', 'tensor')
- grad_in: float32 [2, 2, 4, 1024, 1024], P('section', None, 'dp', 'tensor')
- grad_query: float32 [2, 1024, 1024], P('section', None, 'tensor')
- grad_key: float32 [2, 1024, 1024], P('section', None, 'tensor')
- grad_value: float32 [2, 1024, 1024], P('section', None, 'tensor')
- grad_output: float32 [2, 1024, 1024], P('section', 'tensor')
- grad_qkscale: float32 [2, 1024], P('section', 'tensor')
- grad_attnrate: float32 [2, 1024], P('section')
- grad_up: float32 [2, 1024, 4096], P('section', None, 'tensor')
- grad_gate: float32 [2, 1024, 4096], P('section', None, 'tensor')
- grad_down: float32 [2, 4096, 1024], P('section', 'tensor')
- grad_upscale: float32 [2, 4096], P('section', 'tensor')
- grad_gatescale: float32 [2, 4096], P('section', 'tensor')
- grad_mlprate: float32 [2, 1024], P('section')
The draws below stay inside these ranges and needn't reach their ends.
All inputs are finite; a program needn't handle non-finite values.
Results may differ from the reference program's by a relative error of at most 0.034.
Values may be sent and summed in bfloat16 or wider, within the bound.
No kernel may reach another device: no remote copies, remote signals or barrier semaphores. Data moves between devices by JAX's collectives and lax.ppermute only.
A program may use at most 320 MiB of HBM per device.

```python
import jax
import jax.numpy as jnp
from jax import lax

D = 1024
H = 16
HD = 64
FF = 4096
LENGTH = 1024
MICRO = 2
SEQS = 4


def level_of(stream_key, extent, pieces, least, high):
    loudness = 1.0
    for axis_at, parts in pieces:
        draws = jax.random.uniform(jax.random.fold_in(jax.random.fold_in(stream_key, 6), axis_at), (parts,), jnp.float32, least / len(pieces), high / len(pieces))
        loudness = loudness * jnp.repeat(jnp.exp(draws), extent[axis_at] // parts).reshape((-1,) + (1,) * (len(extent) - 1 - axis_at))
    return loudness


def normal_values(rng, dims, width, limit, pieces=(), dtype=jnp.bfloat16):
    values = jax.random.normal(rng, dims, jnp.float32) * width
    if len(pieces) > 0:
        values = level_of(rng, dims, pieces, -0.22, 0.18) * values
    return jnp.clip(values, min=-limit, max=limit).astype(dtype)


def setup_inputs(seed: int = 0) -> dict:
    key_of = jax.random.split(jax.random.key(seed), 15)
    return {
        "hidden_in": normal_values(key_of[0], (MICRO, SEQS, LENGTH, D), 1.0, 6.0, ((1, 4), (2, 4))),
        "cotangent": normal_values(key_of[1], (MICRO, SEQS, LENGTH, D), 1.0, 6.0, ((1, 4), (2, 4))),
        "query_w": normal_values(key_of[2], (2, D, H * HD), D ** -0.5, 0.1875, ((0, 2), (2, 4))),
        "key_w": normal_values(key_of[3], (2, D, H * HD), D ** -0.5, 0.1875, ((0, 2), (2, 4))),
        "value_w": normal_values(key_of[4], (2, D, H * HD), D ** -0.5, 0.1875, ((0, 2), (2, 4))),
        "output_w": normal_values(key_of[5], (2, H * HD, D), (H * HD) ** -0.5, 0.1875, ((0, 2), (1, 4))),
        "qk_scale": jnp.clip(1.0 + 0.15 * jax.random.normal(key_of[6], (2, H * HD), jnp.float32), 0.25, 1.75),
        "attn_rate": jnp.clip(0.1 + 0.5 * jax.random.uniform(key_of[7], (2, D), jnp.float32) ** level_of(key_of[7], (2, D), ((0, 2),), -0.2, 0.2), 0.1, 0.6),
        "up_w": normal_values(key_of[8], (2, D, FF), D ** -0.5, 0.1875, ((0, 2), (2, 4))),
        "gate_w": normal_values(key_of[9], (2, D, FF), D ** -0.5, 0.1875, ((0, 2), (2, 4))),
        "down_w": normal_values(key_of[10], (2, FF, D), FF ** -0.5, 0.09375, ((0, 2), (1, 4))),
        "up_scale": jnp.clip(1.0 + 0.15 * jax.random.normal(key_of[11], (2, FF), jnp.float32), 0.25, 1.75),
        "gate_scale": jnp.clip(1.0 + 0.15 * jax.random.normal(key_of[12], (2, FF), jnp.float32), 0.25, 1.75),
        "mlp_rate": jnp.clip(0.1 + 0.5 * jax.random.uniform(key_of[13], (2, D), jnp.float32) ** level_of(key_of[13], (2, D), ((0, 2),), -0.2, 0.2), 0.1, 0.6),
    }


@jax.custom_vjp
def low(v):
    return lax.optimization_barrier(v.astype(jnp.bfloat16)).astype(jnp.float32)

@jax.custom_vjp
def low_back(v):
    return v

def low_keep(v):
    return (low(v), None)

def low_pass(kept, grad):
    return (grad,)

def back_keep(v):
    return (v, None)

def back_low(kept, grad):
    return (low(grad),)
low.defvjp(low_keep, low_pass)
low_back.defvjp(back_keep, back_low)
highest = lax.Precision.HIGHEST

def product(left_arr, right_arr):
    return jnp.dot(left_arr, right_arr, precision=highest, preferred_element_type=jnp.float32)

def sphere(values):
    return values * lax.rsqrt(lax.optimization_barrier(jnp.mean(values * values, axis=-1, keepdims=True)) + 1e-06)

def head_sphere(query, scaling):
    head_parts = query.reshape(query.shape[0], -1, HD)
    return sphere(head_parts).reshape(query.shape) * scaling

def blend_rows(hidden, branch, rate_vec):
    return sphere(hidden + rate_vec * (sphere(branch) - hidden))

def attention(query_low, key_low, value_low):
    length = query_low.shape[0]
    query_heads = query_low.reshape(length, -1, HD)
    key_heads = key_low.reshape(length, -1, HD)
    value_heads = value_low.reshape(length, -1, HD)
    scores = jnp.einsum('qhd,khd->hqk', query_heads, key_heads, precision=highest) * HD ** (-0.5)
    scores = low_back(scores)
    causal = jnp.arange(length)[None, :] <= jnp.arange(length)[:, None]
    scores = jnp.where(causal[None], scores, -1e+30)
    weights = low(jax.nn.softmax(scores, axis=-1))
    result = jnp.einsum('hqk,khd->qhd', weights, value_heads, precision=highest)
    return result.reshape(length, -1)

def block_layer(hidden, params):
    query_w, key_w, value_w, output_w, qk_scale, attn_rate, up_w, gate_w, down_w, up_scale, gate_scale, mlp_rate = params
    query_raw = low_back(product(hidden, query_w))
    key_raw = low_back(product(hidden, key_w))
    value_raw = low_back(product(hidden, value_w))
    query_low = low(head_sphere(query_raw, qk_scale))
    key_low = low(head_sphere(key_raw, qk_scale))
    value_low = low(value_raw)
    attended = low(low_back(attention(query_low, key_low, value_low)))
    attn_sum = low_back(product(attended, output_w))
    middle = blend_rows(hidden, attn_sum, attn_rate)
    middle_low = low(middle)
    up_raw = low_back(product(middle_low, up_w))
    gate_raw = low_back(product(middle_low, gate_w))
    inner_low = low(jax.nn.silu(gate_raw * gate_scale) * (up_raw * up_scale))
    mlp_sum = low_back(product(inner_low, down_w))
    return blend_rows(middle, mlp_sum, mlp_rate)

def reference(hidden_in, cotangent, query_w, key_w, value_w, output_w, qk_scale, attn_rate, up_w, gate_w, down_w, up_scale, gate_scale, mlp_rate):
    params = tuple((member.astype(jnp.float32) for member in (query_w, key_w, value_w, output_w, qk_scale, attn_rate, up_w, gate_w, down_w, up_scale, gate_scale, mlp_rate)))
    seq_total = MICRO * SEQS
    inputs = hidden_in.astype(jnp.float32).reshape(seq_total, LENGTH, D)
    probe_zero = jnp.zeros_like(inputs)

    def forward(inputs, probe_zero, params):
        first_params = tuple((member[0] for member in params))
        second_params = tuple((member[1] for member in params))

        def per_seq(seq_pair):
            first_out = block_layer(seq_pair[0], first_params)
            second_out = block_layer(low_back(low(first_out) + seq_pair[1]), second_params)
            return (first_out, second_out)
        return lax.map(jax.checkpoint(per_seq), (inputs, probe_zero))
    (first_out, second_out), pullback = jax.vjp(forward, inputs, probe_zero, params)
    grad_inputs, grad_probe, grad_params = pullback((jnp.zeros_like(first_out), cotangent.astype(jnp.float32).reshape(seq_total, LENGTH, D)))
    full_shape = (MICRO, SEQS, LENGTH, D)
    hidden_out = jnp.stack([first_out.reshape(full_shape), second_out.reshape(full_shape)]).astype(jnp.bfloat16)
    grad_in = jnp.stack([grad_inputs.reshape(full_shape), grad_probe.reshape(full_shape)])
    return (hidden_out, grad_in, grad_params[0], grad_params[1], grad_params[2], grad_params[3], grad_params[4], grad_params[5], grad_params[6], grad_params[7], grad_params[8], grad_params[9], grad_params[10], grad_params[11])
```

```python
import functools

import jax
import jax.numpy as jnp
from jax import lax
from jax.experimental import pallas as pl
from jax.experimental.pallas import tpu as pltpu
from jax.sharding import PartitionSpec as P

HD = 64
EPS = 1e-06
AXES = ("section", "tensor", "dp")
F32 = jnp.float32
LOW = jnp.bfloat16
VMEM_LIMIT = 50 * 1024 * 1024


def cost(flops, bytes_accessed, transcendentals):
    return pl.CostEstimate(flops=0, bytes_accessed=0, transcendentals=0)


class Place:
    def __init__(self, mesh):
        self.sections = mesh.shape["section"]
        self.tensors = mesh.shape["tensor"]
        self.replicas = mesh.shape["dp"]
        self.lanes = self.tensors // 2
        self.pairs = self.replicas // 2
        self.lane_bits = [1 << bit for bit in range(self.lanes.bit_length() - 1)]
        self.pair_bits = [1 << bit for bit in range(self.pairs.bit_length() - 1)]

    def here(self):
        tensor = lax.axis_index("tensor")
        replica = lax.axis_index("dp")
        self.section = lax.axis_index("section")
        self.half = tensor // self.lanes
        self.lane = tensor % self.lanes
        self.pair = replica // 2
        self.core = replica % 2
        self.own = self.half == self.core
        self.first = self.section == 0

    def move(self, value, target):
        def index(section, half, lane, pair, core):
            tensor = half * self.lanes + lane
            return (section * self.tensors + tensor) * self.replicas + pair * 2 + core

        links = []
        for section in range(self.sections):
            for half in range(2):
                for lane in range(self.lanes):
                    for pair in range(self.pairs):
                        for core in range(2):
                            source = (section, half, lane, pair, core)
                            sink = target(*source)
                            if sink is not None:
                                links.append((index(*source), index(*sink)))
        return lax.ppermute(value, AXES, links)

    def across_cores(self, value):
        return self.move(value, lambda s, h, l, p, c: (s, h, l, p, 1 - c))

    def across_lanes(self, value, bit):
        return self.move(value, lambda s, h, l, p, c: (s, h, l ^ bit, p, c))


def to_section(s, h, l, p, c):
    return (1 - s, h, l, p, c)


def to_core(s, h, l, p, c):
    return (s, h, l, p, 1 - c)


def to_half(s, h, l, p, c):
    return (s, 1 - h, l, p, c)


def transposed(s, h, l, p, c):
    return (s, c, l, p, h) if h != c else None


def to_pair(bit):
    return lambda s, h, l, p, c: (s, h, l, p ^ bit, c)


def to_lane(bit):
    return lambda s, h, l, p, c: (s, h, l ^ bit, p, c)


def only(target, test):
    return lambda s, h, l, p, c: target(s, h, l, p, c) if test(s, h, c) else None


class Background:
    def __init__(self, place):
        self.place = place
        self.waiting = []
        self.active = []

    def add(self, task):
        self.waiting.append(task)

    def busy(self):
        return bool(self.waiting or self.active)

    def step(self, anchor, starts=1):
        if not self.busy():
            return anchor
        due = [entry for entry in self.active if entry[2] <= 1]
        kept = [(task, flying, left - 1) for task, flying, left in self.active if left > 1]
        anchor, landed = lax.optimization_barrier((anchor, [flying for _, flying, _ in due]))
        tasks = [(task, arrived) for (task, _, _), arrived in zip(due, landed)]
        for _ in range(starts):
            if self.waiting:
                tasks.append((self.waiting.pop(0), None))
        asked = []
        for task, arrived in tasks:
            try:
                wanted = task.send(arrived)
            except StopIteration:
                continue
            wanted, steps = wanted if isinstance(wanted, tuple) else (wanted, 1)
            asked.append((task, wanted, steps))
        arrays = [[array for array, _ in wanted] for _, wanted, _ in asked]
        anchor, arrays = lax.optimization_barrier((anchor, arrays))
        self.active = kept + [
            (
                task,
                [self.place.move(array, target) for array, (_, target) in zip(ready, wanted)],
                steps,
            )
            for (task, wanted, steps), ready in zip(asked, arrays)
        ]
        return anchor

    def drain(self):
        while self.busy():
            self.step((), 8)


def spec(count):
    return [pl.BlockSpec(memory_space=pltpu.VMEM)] * count


def mean_of(values):
    return jnp.mean(values, axis=-1, keepdims=True)


def load_terms(refs, swaps, lanes):
    total = refs[0][...].astype(F32)
    for ref, bit in zip(refs[1:], swaps[1:]):
        part = ref.shape[0] // lanes
        order = [ref[(at ^ bit) * part : ((at ^ bit) + 1) * part, :] for at in range(lanes)]
        value = order[0] if lanes == 1 else jnp.concatenate(order, axis=0)
        total = total + value.astype(F32)
    return total


def blend_forward(lanes, hidden, branch, rate, out_dtypes):
    rows, width = hidden.shape
    branch, swaps = zip(*branch)

    def kernel(*refs):
        hidden_ref, rate_ref = refs[:2]
        branch_refs = refs[2 : 2 + len(branch)]
        out_refs = refs[2 + len(branch) :]
        h = hidden_ref[...].astype(F32)
        b = load_terms(branch_refs, swaps, lanes)
        mixed = b * lax.rsqrt(mean_of(b * b) + EPS)
        u = h + rate_ref[...] * (mixed - h)
        y = u * lax.rsqrt(mean_of(u * u) + EPS)
        for ref in out_refs:
            ref[...] = y.astype(ref.dtype)

    return pl.pallas_call(
        kernel,
        out_shape=[jax.ShapeDtypeStruct((rows, width), kind) for kind in out_dtypes],
        in_specs=spec(2 + len(branch)),
        out_specs=spec(len(out_dtypes)),
        compiler_params=pltpu.CompilerParams(vmem_limit_bytes=VMEM_LIMIT),
        cost_estimate=cost(
            flops=12 * rows * width, bytes_accessed=10 * rows * width, transcendentals=0
        ),
        name="blend_forward",
    )(hidden, rate, *branch)


def blend_backward(lanes, hidden, branch, rate, grads):
    rows, width = hidden.shape
    branch, branch_swaps = zip(*branch)
    grads, grad_swaps = zip(*grads)
    branches = len(branch)

    def kernel(*refs):
        hidden_ref, rate_ref = refs[:2]
        hidden_out, branch_out, rate_out = refs[-3:]
        h = hidden_ref[...].astype(F32)
        b = load_terms(refs[2 : 2 + branches], branch_swaps, lanes)
        g = load_terms(refs[2 + branches : -3], grad_swaps, lanes)
        a = rate_ref[...]
        root_b = lax.rsqrt(mean_of(b * b) + EPS)
        delta = b * root_b - h
        u = h + a * delta
        root_u = lax.rsqrt(mean_of(u * u) + EPS)
        grad_u = root_u * g - u * (root_u * root_u * root_u * mean_of(u * g))
        grad_mixed = grad_u * a
        hidden_out[...] = grad_u - grad_mixed
        rate_out[...] = jnp.sum(grad_u * delta, axis=0, keepdims=True)
        grad_b = root_b * grad_mixed - b * (
            root_b * root_b * root_b * mean_of(b * grad_mixed)
        )
        branch_out[...] = grad_b.astype(branch_out.dtype)

    return pl.pallas_call(
        kernel,
        out_shape=[
            jax.ShapeDtypeStruct((rows, width), F32),
            jax.ShapeDtypeStruct((rows, width), LOW),
            jax.ShapeDtypeStruct((1, width), F32),
        ],
        in_specs=spec(2 + branches + len(grads)),
        out_specs=spec(3),
        compiler_params=pltpu.CompilerParams(vmem_limit_bytes=VMEM_LIMIT),
        cost_estimate=cost(
            flops=30 * rows * width, bytes_accessed=20 * rows * width, transcendentals=0
        ),
        name="blend_backward",
    )(hidden, rate, *branch, *grads)


def head_masks(width):
    lanes = lax.broadcasted_iota(jnp.int32, (1, width), 1)
    return [
        (lanes >= head * HD) & (lanes < (head + 1) * HD) for head in range(width // HD)
    ]


def head_mean(values, masks):
    if len(masks) == 1:
        return jnp.sum(values, axis=-1, keepdims=True) * (1.0 / HD)
    result = None
    for mask in masks:
        total = jnp.sum(jnp.where(mask, values, 0.0), axis=-1, keepdims=True) * (1.0 / HD)
        result = total if result is None else jnp.where(mask, total, result)
    return result


def nt_dot(left, right):
    return lax.dot_general(left, right, (((1,), (1,)), ((), ())), preferred_element_type=F32)


def tn_dot(left, right):
    return lax.dot_general(left, right, (((0,), (0,)), ((), ())), preferred_element_type=F32)


def nn_dot(left, right):
    return lax.dot_general(left, right, (((1,), (0,)), ((), ())), preferred_element_type=F32)


def fused_dot(xs, used, tiled, outs, epilogue, tile, name, keep=None, at=0, count=1, total=None):
    rows = sum(piece.shape[0] for piece in xs[0])
    outer = used[0][3][0] if len(used[0]) > 3 else used[0][1].shape[0 if used[0][2] else 1]
    tile = min(tile, outer)
    steps = outer // tile
    operands, in_specs = [], []

    def whole(array):
        operands.append(array)
        in_specs.append(pl.BlockSpec(array.shape, lambda i: (0, 0)))

    for pieces in xs:
        for piece in pieces:
            whole(piece)
    for _, weight, flipped, *place in used:
        operands.append(weight)
        begin = place[0][1] if place else 0
        if flipped:
            in_specs.append(pl.BlockSpec((tile, weight.shape[1]), lambda i: (i, 0)))
        else:
            in_specs.append(
                pl.BlockSpec((weight.shape[0], tile), lambda i, begin=begin: (0, begin + i))
            )
    for array, stacked in tiled:
        operands.append(array)
        if stacked:
            in_specs.append(pl.BlockSpec((rows, tile), lambda i: (at, i)))
        else:
            in_specs.append(pl.BlockSpec((array.shape[0], tile), lambda i: (0, i)))
    total_weights = total[0] if total else []
    for weight, flipped in total_weights:
        operands.append(weight)
        if flipped:
            in_specs.append(pl.BlockSpec((weight.shape[0], tile), lambda i: (0, i)))
        else:
            in_specs.append(pl.BlockSpec((tile, weight.shape[1]), lambda i: (i, 0)))
    out_shape, out_specs, aliases, behind = [], [], {}, []

    def stacked_out(kind, columns, block, index, stack):
        if stack:
            aliases[len(operands) + len(behind)] = len(out_shape)
            behind.append(stack[-1])
        out_shape.append(jax.ShapeDtypeStruct((rows * count, columns), kind))
        out_specs.append(pl.BlockSpec(block, index))

    for out_rows, kind, stack in outs:
        if stack is None:
            out_shape.append(jax.ShapeDtypeStruct((out_rows, outer), kind))
            out_specs.append(pl.BlockSpec((out_rows, tile), lambda i: (0, i)))
        else:
            stacked_out(kind, outer, (rows, tile), lambda i: (at, i), stack)
    inner = xs[0][0].shape[1]
    if keep is not None:
        stacked_out(LOW, inner, (rows, inner), lambda i: (at, 0), keep)
    pieces_out = 0
    scratch = []
    if total:
        weight, flipped = total_weights[0]
        columns = weight.shape[0 if flipped else 1]
        pieces_out = 2
        for _ in range(2):
            out_shape.append(jax.ShapeDtypeStruct((rows // 2, columns), LOW))
            out_specs.append(pl.BlockSpec((rows // 2, columns), lambda i: (0, 0)))
        scratch.append(pltpu.VMEM((rows, columns), F32))
    counts = [len(pieces) for pieces in xs]

    def kernel(*refs):
        refs = list(refs)

        def take(number):
            taken, refs[:number] = refs[:number], []
            return taken

        x_refs = [take(number) for number in counts]
        weight_refs = take(len(used))
        tiled_refs = take(len(tiled))
        total_refs = take(len(total_weights))
        take(len(behind))
        out_refs = take(len(outs))
        keep_ref = take(1)[0] if keep is not None else None
        piece_refs = take(pieces_out)
        step = pl.program_id(0)
        if keep_ref is not None:

            @pl.when(step == 0)
            def _():
                start = 0
                for ref in x_refs[0]:
                    keep_ref[start : start + ref.shape[0], :] = ref[...]
                    start += ref.shape[0]

        values = [keep_ref if at_x == 0 and keep_ref is not None else members[0]
                  for at_x, members in enumerate(x_refs)]
        dots = [
            (nt_dot if flipped else nn_dot)(values[which][...], ref[...])
            for (which, _, flipped, *_), ref in zip(used, weight_refs)
        ]
        results, terms = epilogue(dots, [ref[...] for ref in tiled_refs])
        for ref, result in zip(out_refs, results):
            ref[...] = result.astype(ref.dtype)
        if total:
            sum_ref = refs[0]
            term = None
            for (_, flipped), ref, value in zip(total_weights, total_refs, terms):
                product = (nt_dot if flipped else nn_dot)(value, ref[...])
                term = product if term is None else term + product

            @pl.when(step == 0)
            def _():
                sum_ref[...] = term

            @pl.when(step > 0)
            def _():
                sum_ref[...] += term

            @pl.when(step == steps - 1)
            def _():
                start = 0
                for ref in piece_refs:
                    ref[...] = sum_ref[start : start + ref.shape[0], :].astype(LOW)
                    start += ref.shape[0]

    flops = sum(2 * rows * weight.shape[0] * weight.shape[1] for _, weight, *_ in used)
    flops += sum(2 * rows * weight.shape[0] * weight.shape[1] for weight, _ in total_weights)
    moved = sum(array.size * array.dtype.itemsize for array in operands)
    results = pl.pallas_call(
        kernel,
        grid=(steps,),
        out_shape=out_shape,
        in_specs=in_specs + [pl.BlockSpec(memory_space=pl.ANY)] * len(behind),
        out_specs=out_specs,
        scratch_shapes=scratch,
        input_output_aliases=aliases,
        compiler_params=pltpu.CompilerParams(
            vmem_limit_bytes=VMEM_LIMIT, dimension_semantics=("arbitrary",)
        ),
        cost_estimate=cost(flops=flops, bytes_accessed=2 * moved, transcendentals=0),
        name=name,
    )(*operands, *behind)
    results = list(results)
    for (_, _, stack), result in zip(outs, results):
        if stack is not None:
            stack.append(result)
    if keep is not None:
        keep.append(results[len(outs)])
    return results[: len(outs)], results[len(results) - pieces_out :]


def project(pieces, packed, width, at, count, keep):
    rows = sum(piece.shape[0] for piece in pieces)
    used = 3 * width if width % 128 == 0 else 4 * width
    results, _ = fused_dot(
        [pieces],
        [(0, packed, False, (used, 0))],
        [],
        [(rows, F32, None)],
        lambda dots, _: (dots, None),
        width if width % 128 == 0 else used,
        "project",
        keep=keep,
        at=at,
        count=count,
    )
    return results[0]


def mlp_forward(pieces, weights, scales, at, count, stacks):
    up_w, gate_w, down_w = weights
    rows = sum(piece.shape[0] for piece in pieces)

    def epilogue(dots, tiles):
        up_raw, gate_raw = dots
        up_scale, gate_scale = tiles
        gated = gate_raw * gate_scale
        inner = (gated / (1.0 + jnp.exp(-gated)) * (up_raw * up_scale)).astype(LOW)
        return [up_raw, gate_raw, inner], [inner]

    mid, up_raw, gate_raw, inner = stacks
    _, out = fused_dot(
        [pieces],
        [(0, up_w, False), (0, gate_w, False)],
        [(scales[0], False), (scales[1], False)],
        [(rows, LOW, up_raw), (rows, LOW, gate_raw), (rows, LOW, inner)],
        epilogue,
        256,
        "mlp_forward",
        keep=mid,
        at=at,
        count=count,
        total=([(down_w, False)], None),
    )
    return out


def mlp_backward(pieces, weights, scales, raws, at, count, stacks):
    up_w, gate_w, down_w = weights
    rows = sum(piece.shape[0] for piece in pieces)

    def epilogue(dots, tiles):
        up_raw, gate_raw, up_scale, gate_scale = tiles
        up_raw, gate_raw = up_raw.astype(F32), gate_raw.astype(F32)
        grad = dots[0]
        gated = gate_raw * gate_scale
        sigmoid = 1.0 / (1.0 + jnp.exp(-gated))
        silu = gated * sigmoid
        slope = sigmoid * (1.0 + gated * (1.0 - sigmoid))
        from_up = grad * silu
        from_gate = grad * (up_raw * up_scale) * slope
        up_back = (from_up * up_scale).astype(LOW)
        gate_back = (from_gate * gate_scale).astype(LOW)
        up_sum = jnp.sum(from_up * up_raw, axis=0, keepdims=True)
        gate_sum = jnp.sum(from_gate * gate_raw, axis=0, keepdims=True)
        return [up_back, gate_back, up_sum, gate_sum], [up_back, gate_back]

    full, up_back, gate_back = stacks
    results, out = fused_dot(
        [pieces],
        [(0, down_w, True)],
        [(raws[0], True), (raws[1], True), (scales[0], False), (scales[1], False)],
        [(rows, LOW, up_back), (rows, LOW, gate_back), (1, F32, None), (1, F32, None)],
        epilogue,
        256,
        "mlp_backward",
        keep=full,
        at=at,
        count=count,
        total=([(up_w, True), (gate_w, True)], None),
    )
    return results[2], results[3], out


def output_backward(pieces, output_w, at, count, keep):
    rows = sum(piece.shape[0] for piece in pieces)
    results, _ = fused_dot(
        [pieces],
        [(0, output_w, True)],
        [],
        [(rows, LOW, None)],
        lambda dots, _: (dots, None),
        256,
        "output_backward",
        keep=keep,
        at=at,
        count=count,
    )
    return results[0]


def block_starts(places_ref, blocks, part):
    return [
        (block, pl.multiple_of(places_ref[block] * part, part)) for block in range(blocks)
    ]


def load_heads(starts, part, width, gain, masks, raw_ref, query, key, value):
    for block, start in starts:
        rows = pl.ds(block * part, part)
        place = pl.ds(start, part)
        raw = raw_ref[rows, 0:width]
        root = lax.rsqrt(head_mean(raw * raw, masks) + EPS)
        query[place, :] = (raw * root * gain).astype(LOW) * LOW(HD ** (-0.5))
        raw = raw_ref[rows, width : 2 * width]
        root = lax.rsqrt(head_mean(raw * raw, masks) + EPS)
        key[place, :] = (raw * root * gain).astype(LOW)
        value[place, :] = raw_ref[rows, 2 * width : 3 * width].astype(LOW)


def whole_spec(array):
    return pl.BlockSpec(array.shape, lambda i: (0, 0))


def stacked_specs(stack, operands):
    if not stack:
        return [], [], {}
    return [stack[-1]], [pl.BlockSpec(memory_space=pl.ANY)], {operands: 0}


def attention_forward(places, scale, raw, output_w, at, count, stack):
    width = scale.shape[1]
    blocks = places.shape[0]
    length = raw.shape[0]
    part = length // blocks
    span = min(256, length)
    model = output_w.shape[1]
    behind, behind_specs, aliases = stacked_specs(stack, 4)

    def kernel(*refs):
        places_ref, scale_ref, output_ref, raw_ref = refs[:4]
        attended_ref, mine_ref, theirs_ref, query, key, value, result = refs[4 + len(behind) :]
        masks = head_masks(width)
        starts = block_starts(places_ref, blocks, part)
        load_heads(starts, part, width, scale_ref[...], masks, raw_ref, query, key, value)
        row_at = lax.broadcasted_iota(jnp.int32, (span, span), 0)
        col_at = lax.broadcasted_iota(jnp.int32, (span, span), 1)
        causal = col_at <= row_at
        for begin in range(0, length, span):
            rows = query[begin : begin + span, :]
            total = None
            for mask in masks:
                picked = jnp.where(mask, rows, LOW(0))
                last = nt_dot(picked, key[begin : begin + span, :])
                last = jnp.where(causal, jnp.exp(last), 0.0)
                weight = jnp.sum(last, axis=-1, keepdims=True)
                head = nn_dot(last.astype(LOW), value[begin : begin + span, :])
                if begin > 0:
                    first = jnp.exp(nt_dot(picked, key[0:begin, :]))
                    weight = weight + jnp.sum(first, axis=-1, keepdims=True)
                    head = head + nn_dot(first.astype(LOW), value[0:begin, :])
                head = head * (1.0 / weight)
                total = head if total is None else jnp.where(mask, head, total)
            result[begin : begin + span, :] = total.astype(LOW)
        for block, start in starts:
            attended_ref[block * part : (block + 1) * part, :] = result[pl.ds(start, part), :]
        half = length // 2
        mine_ref[...] = nn_dot(attended_ref[:half, :], output_ref[...]).astype(LOW)
        theirs_ref[...] = nn_dot(attended_ref[half:, :], output_ref[...]).astype(LOW)

    attended, mine, theirs = pl.pallas_call(
        kernel,
        grid=(1,),
        out_shape=[
            jax.ShapeDtypeStruct((length * count, width), LOW),
            jax.ShapeDtypeStruct((length // 2, model), LOW),
            jax.ShapeDtypeStruct((length // 2, model), LOW),
        ],
        in_specs=[pl.BlockSpec(memory_space=pltpu.SMEM)]
        + [whole_spec(array) for array in (scale, output_w, raw)]
        + behind_specs,
        out_specs=[pl.BlockSpec((length, width), lambda i: (at, 0))]
        + [pl.BlockSpec((length // 2, model), lambda i: (0, 0))] * 2,
        scratch_shapes=[pltpu.VMEM((length, width), LOW)] * 4,
        input_output_aliases=aliases,
        compiler_params=pltpu.CompilerParams(vmem_limit_bytes=VMEM_LIMIT),
        cost_estimate=cost(
            flops=8 * length * length * width,
            bytes_accessed=24 * length * width,
            transcendentals=length * length * (width // HD),
        ),
        name="attention_forward",
    )(places, scale, output_w, raw, *behind)
    stack.append(attended)
    return mine, theirs


def attention_backward(places, scale, raw, grads, packed, at, count, stack):
    width = scale.shape[1]
    blocks = places.shape[0]
    length = raw.shape[0]
    part = length // blocks
    span = min(256, length)
    model = packed.shape[0]
    behind, behind_specs, aliases = stacked_specs(stack, 5)

    def kernel(*refs):
        places_ref, scale_ref, packed_ref, raw_ref, grad_ref = refs[:5]
        back_ref, scale_out, mine_ref, theirs_ref = refs[5 + len(behind) : 9 + len(behind)]
        query, key, value, grad, query_sum, key_sum, value_sum = refs[9 + len(behind) :]
        masks = head_masks(width)
        gain = scale_ref[...]
        starts = block_starts(places_ref, blocks, part)
        load_heads(starts, part, width, gain, masks, raw_ref, query, key, value)
        for block, start in starts:
            grad[pl.ds(start, part), :] = grad_ref[block * part : (block + 1) * part, :]
        key_sum[...] = jnp.zeros_like(key_sum)
        value_sum[...] = jnp.zeros_like(value_sum)
        key_at = lax.broadcasted_iota(jnp.int32, (span, span), 0)
        query_at = lax.broadcasted_iota(jnp.int32, (span, span), 1)
        causal = key_at <= query_at
        for origin in range(0, length, span):
            rows = query[origin : origin + span, :]
            grad_rows = grad[origin : origin + span, :]
            total = None
            for mask in masks:
                picked = jnp.where(mask, rows, LOW(0))
                grad_picked = jnp.where(mask, grad_rows, LOW(0))
                pieces = [slice(0, origin)] if origin > 0 else []
                pieces.append(slice(origin, origin + span))
                raised = [jnp.exp(nt_dot(key[piece, :], picked)) for piece in pieces]
                raised[-1] = jnp.where(causal, raised[-1], 0.0)
                weight = sum(jnp.sum(member, axis=0, keepdims=True) for member in raised)
                inverse = 1.0 / weight
                probs = [member * inverse for member in raised]
                grad_probs = [nt_dot(value[piece, :], grad_picked) for piece in pieces]
                row_sum = sum(
                    jnp.sum(left * right, axis=0, keepdims=True)
                    for left, right in zip(probs, grad_probs)
                )
                head = None
                for piece, prob, grad_prob in zip(pieces, probs, grad_probs):
                    grad_score = (prob * (grad_prob - row_sum)).astype(LOW)
                    value_sum[piece, :] += nn_dot(prob.astype(LOW), grad_picked)
                    key_sum[piece, :] += nn_dot(grad_score, picked)
                    term = tn_dot(grad_score, key[piece, :])
                    head = term if head is None else head + term
                total = head if total is None else jnp.where(mask, head, total)
            query_sum[origin : origin + span, :] = total * (HD ** (-0.5))
        scale_sum = jnp.zeros((1, width), F32)
        for block, start in starts:
            rows = slice(block * part, (block + 1) * part)
            place = pl.ds(start, part)
            for slot, source in ((0, query_sum), (1, key_sum)):
                lanes = slice(slot * width, (slot + 1) * width)
                raw_rows = raw_ref[rows, lanes]
                root = lax.rsqrt(head_mean(raw_rows * raw_rows, masks) + EPS)
                grad_low = source[place, :]
                scale_sum = scale_sum + jnp.sum(
                    grad_low * (raw_rows * root), axis=0, keepdims=True
                )
                grad_unit = grad_low * gain
                cross = head_mean(raw_rows * grad_unit, masks)
                result = root * grad_unit - raw_rows * (root * root * root * cross)
                back_ref[rows, lanes] = result.astype(LOW)
            back_ref[rows, 2 * width : 3 * width] = value_sum[place, :].astype(LOW)
        scale_out[...] = scale_sum
        half = length // 2
        weights = packed_ref[:, : 3 * width]
        mine_ref[...] = nt_dot(back_ref[:half, :], weights).astype(LOW)
        theirs_ref[...] = nt_dot(back_ref[half:, :], weights).astype(LOW)

    back, scale_sum, mine, theirs = pl.pallas_call(
        kernel,
        grid=(1,),
        out_shape=[
            jax.ShapeDtypeStruct((length * count, 3 * width), LOW),
            jax.ShapeDtypeStruct((1, width), F32),
            jax.ShapeDtypeStruct((length // 2, model), LOW),
            jax.ShapeDtypeStruct((length // 2, model), LOW),
        ],
        in_specs=[pl.BlockSpec(memory_space=pltpu.SMEM)]
        + [whole_spec(array) for array in (scale, packed, raw, grads)]
        + behind_specs,
        out_specs=[
            pl.BlockSpec((length, 3 * width), lambda i: (at, 0)),
            pl.BlockSpec((1, width), lambda i: (0, 0)),
        ]
        + [pl.BlockSpec((length // 2, model), lambda i: (0, 0))] * 2,
        scratch_shapes=[pltpu.VMEM((length, width), LOW)] * 4
        + [pltpu.VMEM((length, width), F32)] * 3,
        input_output_aliases=aliases,
        compiler_params=pltpu.CompilerParams(vmem_limit_bytes=VMEM_LIMIT),
        cost_estimate=cost(
            flops=20 * length * length * width,
            bytes_accessed=32 * length * width,
            transcendentals=length * length * (width // HD),
        ),
        name="attention_backward",
    )(places, scale, packed, raw, grads, *behind)
    stack.append(back)
    return scale_sum, mine, theirs


def gather(place, value):
    half = value.shape[0] // 2
    return [value, place.across_cores(value[:half]), place.across_cores(value[half:])]


def gather_lanes(place, value):
    rows = [value]
    for bit in place.lane_bits:
        rows = rows + [place.across_lanes(member, bit) for member in rows]
    return jnp.concatenate(rows, axis=0)


def exchange(place, total):
    terms = [(total, 0)]
    for bit in place.lane_bits:
        total = terms[0][0]
        for value, swapped in terms[1:]:
            total = plus(total, unswapped(place, value, swapped))
        terms = [(total, 0), (place.across_lanes(total, bit), bit)]
    return terms


def unswapped(place, value, bit):
    part = value.shape[0] // place.lanes
    order = [value[(at ^ bit) * part : ((at ^ bit) + 1) * part] for at in range(place.lanes)]
    return jnp.concatenate(order, axis=0)


def spread_task(place, name, shard, steps, ready):
    rows = shard.shape[0] // place.pairs
    cut = lax.dynamic_slice_in_dim(shard, place.pair * rows, rows, 0)
    parts = yield [(cut, only(to_half, lambda s, h, c: c == h))], steps
    for bit in place.pair_bits:
        got = yield [(part, only(to_pair(bit), lambda s, h, c: c != h)) for part in parts]
        parts = parts + got
    ready[name] = assemble(place, shard, parts)


def assemble(place, shard, parts):
    pairs = place.pairs
    flags = jnp.stack([place.own.astype(jnp.int32), place.pair])

    def kernel(flags_ref, own_ref, *refs):
        part_refs, out_ref, sems = refs[:pairs], refs[pairs], refs[-1]

        @pl.when(flags_ref[0] == 1)
        def _():
            copy = pltpu.make_async_copy(own_ref, out_ref, sems.at[0])
            copy.start()
            copy.wait()

        @pl.when(flags_ref[0] == 0)
        def _():
            copies = []
            for step in range(pairs):
                rows = part_refs[step].shape[0]
                begin = pl.multiple_of((flags_ref[1] ^ step) * rows, rows)
                sink = out_ref.at[pl.ds(begin, rows), :]
                copies.append(pltpu.make_async_copy(part_refs[step], sink, sems.at[step]))
            for copy in copies:
                copy.start()
            for copy in copies:
                copy.wait()

    return pl.pallas_call(
        kernel,
        out_shape=jax.ShapeDtypeStruct(shard.shape, shard.dtype),
        in_specs=[pl.BlockSpec(memory_space=pltpu.SMEM)]
        + [pl.BlockSpec(memory_space=pl.ANY)] * (1 + pairs),
        out_specs=pl.BlockSpec(memory_space=pltpu.VMEM),
        scratch_shapes=[pltpu.SemaphoreType.DMA((pairs,))],
        compiler_params=pltpu.CompilerParams(vmem_limit_bytes=VMEM_LIMIT),
        cost_estimate=cost(
            flops=0, bytes_accessed=4 * shard.size, transcendentals=0
        ),
        name="assemble",
    )(flags, shard, *parts)


def halved(value, bit, rows):
    half = rows // 2
    kept = lax.dynamic_slice_in_dim(value, bit * half, half, 0)
    sent = lax.dynamic_slice_in_dim(value, (1 - bit) * half, half, 0)
    return kept, sent


def plus(left, right):
    return (left.astype(F32) + right.astype(F32)).astype(LOW)


def collect_task(place, grad, store):
    held = grad
    for bit in place.pair_bits[::-1]:
        kept, sent = halved(held, (place.pair // bit) % 2, held.shape[0])
        (met,) = yield [(sent, to_pair(bit))]
        held = plus(kept, met)
    (met,) = yield [(held, only(to_half, lambda s, h, c: c != h))]
    held = plus(held, met)
    parts = [held]
    for bit in place.pair_bits:
        got = yield [(value, only(to_pair(bit), lambda s, h, c: c == h)) for value in parts]
        parts = parts + got
    got = yield [(value, only(to_core, lambda s, h, c: c == h)) for value in parts]
    store.append((parts, got))


def finish(place, sides, shape, columns):
    pairs = place.pairs
    rows, width = shape
    piece = rows // pairs
    flags = jnp.stack([place.own.astype(jnp.int32), place.pair])
    operands = [member for side in sides for member in side]

    def kernel(flags_ref, *refs):
        part_refs = refs[: len(operands)]
        out_refs = refs[len(operands) : -2]
        landing, sems = refs[-2:]
        step = pl.program_id(0)

        @pl.when(step == 0)
        def _():
            for side in range(2):

                @pl.when(flags_ref[0] == 1 - side)
                def _():
                    for relative in range(pairs):
                        block = flags_ref[1] ^ relative
                        pltpu.make_async_copy(
                            part_refs[side * pairs + relative],
                            landing.at[block],
                            sems.at[block],
                        ).start()

        pltpu.make_async_copy(part_refs[0], landing.at[step], sems.at[step]).wait()
        value = landing[step].astype(F32)
        begin = 0
        for count, ref in zip(columns, out_refs):
            ref[...] = value[:, begin : begin + count]
            begin += count

    return pl.pallas_call(
        kernel,
        grid=(pairs,),
        out_shape=[jax.ShapeDtypeStruct((rows, count), F32) for count in columns],
        in_specs=[pl.BlockSpec(memory_space=pltpu.SMEM)]
        + [pl.BlockSpec(memory_space=pl.ANY)] * len(operands),
        out_specs=[pl.BlockSpec((piece, count), lambda i: (i, 0)) for count in columns],
        scratch_shapes=[
            pltpu.VMEM((pairs, piece, width), LOW),
            pltpu.SemaphoreType.DMA((pairs,)),
        ],
        compiler_params=pltpu.CompilerParams(
            vmem_limit_bytes=VMEM_LIMIT, dimension_semantics=("arbitrary",)
        ),
        cost_estimate=cost(
            flops=0, bytes_accessed=6 * rows * width, transcendentals=0
        ),
        name="finish",
    )(flags, *operands)


def move_task(place, value, target, store, steps=1):
    (met,) = yield [(value, target)], steps
    store.append(jnp.where(place.own, value, met))


def small_task(place, small, rates, store):
    count = small.shape[1]
    slots = jnp.concatenate(
        [jnp.where(place.core == slot, small, 0.0) for slot in range(2)] + [rates], axis=1
    )
    targets = [to_core, to_half] + [to_pair(bit) for bit in place.pair_bits]
    for target in targets:
        (met,) = yield [(slots, target)]
        slots = slots + met
    store.append(jnp.where(place.half == 0, slots[:, :count], slots[:, count : 2 * count]))
    store.append(slots[:, 2 * count :])


class Weights:
    def __init__(self, bg, width, ready):
        self.bg, self.width, self.ready = bg, width, ready

    def wait(self, names, anchor):
        while any(name not in self.ready for name in names):
            anchor = self.bg.step(anchor)
        if "out" not in self.ready:
            self.ready["out"] = self.ready["attn"][:, 3 * self.width :].T
        return anchor

    def __getitem__(self, name):
        return self.ready[name]


class Chain:
    def __init__(self, place, bg):
        self.place, self.bg = place, bg
        self.last = None
        self.ready = None

    def exchange(self, mine, theirs, starts=None):
        if self.last:
            flying = [value for value, _ in self.last]
            theirs, flying = lax.optimization_barrier((theirs, flying))
            self.last[:] = [(value, bit) for value, (_, bit) in zip(flying, self.last)]
        if starts is not None:
            theirs = self.bg.step(theirs, starts)
        self.ready = plus(mine, self.place.across_cores(theirs))
        self.last = []
        return self.last

    def after(self, values):
        if self.ready is not None:
            values, total = lax.optimization_barrier((values, self.ready))
            self.ready = None
            self.last[:] = exchange(self.place, total)
        return values

    def terms_after(self, terms):
        if terms is self.last and self.ready is not None:
            self.after([])
        values = self.after([value for value, _ in terms])
        return [(value, bit) for value, (_, bit) in zip(values, terms)]


def layer_forward(place, places, bg, chain, rows, weights, scales, late=None):
    qk_scale, attn_rate, up_scale, gate_scale, mlp_rate = scales
    width = qk_scale.shape[1]
    count = late[1] if late else len(rows)
    streams = range(count)
    lanes = place.lanes
    full_in, attended, raws, attn_terms = [], [], [], []
    for at in streams:
        if at == len(rows):
            rows.append(gather_lanes(place, chain.after(late[0][at])))
        pieces = chain.after(gather(place, rows[at]))
        pieces = weights.wait(("attn",), pieces)
        raws.append(project(pieces, weights["attn"], width, at, count, full_in))
        mine, theirs = attention_forward(
            places, qk_scale, raws[at], weights["out"], at, count, attended
        )
        attn_terms.append(chain.exchange(mine, theirs, 1))
    middles, mlp_terms, results = [], [], []
    stacks = [[], [], [], []]
    for at in streams:
        terms = chain.terms_after(attn_terms[at])
        middles.append(blend_forward(lanes, rows[at], terms, attn_rate, [F32, LOW]))
        pieces = gather(place, middles[at][1])
        pieces = weights.wait(("up", "gate", "down"), pieces)
        mine, theirs = mlp_forward(
            pieces,
            (weights["up"], weights["gate"], weights["down"]),
            (up_scale, gate_scale),
            at,
            count,
            stacks,
        )
        mlp_terms.append(chain.exchange(mine, theirs))
    for at in streams:
        results.append(
            blend_forward(
                lanes, middles[at][0], chain.terms_after(mlp_terms[at]), mlp_rate, [LOW]
            )[0]
        )
    kept = (rows, full_in[-1], raws, attended[-1], attn_terms, middles, stacks, mlp_terms)
    return results, kept


def layer_backward(place, places, chain, grads, kept, weights, scales, collect, starts):
    rows, full_in, raws, attended, attn_terms, middles, stacks, mlp_terms = kept
    full_mid, up_raw, gate_raw, inner = (stack[-1] for stack in stacks)
    qk_scale, attn_rate, up_scale, gate_scale, mlp_rate = scales
    count = len(rows)
    streams = range(count)
    lanes = place.lanes

    mlp_back, sums, mid_terms = [], [], []
    back_stacks = [[], [], []]
    for at in streams:
        terms = chain.terms_after(grads[at])
        mlp_back.append(
            blend_backward(lanes, middles[at][0], mlp_terms[at], mlp_rate, terms)
        )
        pieces = gather(place, mlp_back[at][1])
        up_sum, gate_sum, (mine, theirs) = mlp_backward(
            pieces,
            (weights["up"], weights["gate"], weights["down"]),
            (up_scale, gate_scale),
            (up_raw, gate_raw),
            at,
            count,
            back_stacks,
        )
        sums.append((up_sum, gate_sum))
        mid_terms.append(chain.exchange(mine, theirs, starts[at]))
    full_mlp, up_back, gate_back = chain.after([stack[-1] for stack in back_stacks])
    collect("down", tn_dot(inner, full_mlp).astype(LOW))
    collect("up", tn_dot(full_mid, up_back).astype(LOW))
    collect("gate", tn_dot(full_mid, gate_back).astype(LOW))
    attn_back, full_attn, back, in_terms, qk_sums = [], [], [], [], []
    for at in streams:
        terms = chain.terms_after([(mlp_back[at][0], 0)] + mid_terms[at])
        attn_back.append(blend_backward(lanes, rows[at], attn_terms[at], attn_rate, terms))
        pieces = gather(place, attn_back[at][1])
        grad_attended = output_backward(pieces, weights["out"], at, count, full_attn)
        qk_sum, mine, theirs = attention_backward(
            places, qk_scale, raws[at], grad_attended, weights["attn"], at, count, back
        )
        qk_sums.append(qk_sum)
        in_terms.append(chain.exchange(mine, theirs, starts[count + at]))
    last = chain.after(back[-1])
    collect(
        "attn",
        jnp.concatenate(
            [tn_dot(full_in, last), tn_dot(full_attn[-1], attended)], axis=1
        ).astype(LOW),
    )
    small = jnp.concatenate(
        [sum(qk_sums), sum(member[0] for member in sums), sum(member[1] for member in sums)],
        axis=1,
    )
    rates = jnp.concatenate(
        [sum(member[2] for member in attn_back), sum(member[2] for member in mlp_back)], axis=1
    )
    grad_rows = [[(attn_back[at][0], 0)] + in_terms[at] for at in streams]
    return grad_rows, small, rates


def body(place, *args):
    (
        hidden_in,
        cotangent,
        query_w,
        key_w,
        value_w,
        output_w,
        qk_scale,
        attn_rate,
        up_w,
        gate_w,
        down_w,
        up_scale,
        gate_scale,
        mlp_rate,
    ) = args
    place.here()
    first = place.first
    width, units = query_w.shape[2], up_w.shape[2]
    part = hidden_in.shape[2]
    streams = range(hidden_in.shape[0])
    bg = Background(place)
    chain = Chain(place, bg)

    shards = {
        "attn": jnp.concatenate([query_w[0], key_w[0], value_w[0], output_w[0].T], axis=1),
        "up": up_w[0],
        "gate": gate_w[0],
        "down": down_w[0],
    }
    ready = {}

    small_in = jnp.concatenate([qk_scale, up_scale, gate_scale], axis=1)
    start_rows, small_rows = [], []
    start = [jnp.where(first, hidden_in[at, 0], cotangent[at, 0]) for at in streams]
    bg.add(move_task(place, start[0], transposed, start_rows))
    bg.add(move_task(place, small_in, only(to_half, lambda s, h, c: c == h), small_rows))
    bg.add(spread_task(place, "attn", shards["attn"], 1, ready))
    for member in start[1:]:
        bg.add(move_task(place, member, transposed, start_rows, 2))
    for name in ("up", "gate", "down"):
        bg.add(spread_task(place, name, shards[name], 2, ready))
    bg.step((), 3)
    bg.step((), len(start))
    start = [gather_lanes(place, start_rows[0])]
    edges = [0, width, width + units, width + 2 * units]
    qk, up, gate = (small_rows[0][:, a:b] for a, b in zip(edges[:3], edges[1:]))
    scales = (qk, attn_rate, up, gate, mlp_rate)
    weights = Weights(bg, width, ready)

    blocks = [
        (place.core ^ other) * place.lanes + (place.lane ^ step)
        for other in range(2)
        for step in range(place.lanes)
    ]
    places = jnp.stack(blocks).astype(jnp.int32)

    def own_rows(members):
        return jnp.stack([member[:part] for member in members])

    def hop(value, source):
        return place.move(value, only(to_section, lambda s, h, c: s == source))

    def summed(terms):
        total = terms[0][0].astype(F32)
        for value, bit in terms[1:]:
            total = total + (unswapped(place, value, bit) if bit else value).astype(F32)
        return total.astype(LOW)

    first_out, kept_first = layer_forward(
        place, places, bg, chain, start, weights, scales, (start_rows, len(streams))
    )
    second_in = [hop(member, 0) for member in first_out]
    second_out, kept_second = layer_forward(place, places, bg, chain, second_in, weights, scales)
    hidden_out, grad_in, sums = [], [], []
    late = {}
    grad_mid, second_small, second_rates = layer_backward(
        place,
        places,
        chain,
        [[(member, 0)] for member in start],
        kept_second,
        weights,
        scales,
        late.__setitem__,
        [None] * (2 * len(streams)),
    )
    grad_second = [summed(terms) for terms in grad_mid]
    grad_back = [hop(member, 1) for member in grad_second]
    stores = {name: [] for name in shards}

    def collect(name, grad):
        mine = jnp.where(first, grad, late[name])
        bg.add(collect_task(place, mine, stores[name]))

    grad_start, first_small, first_rates = layer_backward(
        place,
        places,
        chain,
        [[(member, 0)] for member in grad_back],
        kept_first,
        weights,
        scales,
        collect,
        [None] * len(streams) + [2] + [1] * (len(streams) - 1),
    )
    grad_first = [summed(terms) for terms in grad_start]
    bg.add(
        small_task(
            place,
            jnp.where(first, first_small, second_small),
            jnp.where(first, first_rates, second_rates),
            sums,
        )
    )
    in_rows = jnp.where(first, own_rows(grad_first), own_rows(grad_second))
    bg.add(move_task(place, in_rows, transposed, grad_in))
    out_rows = jnp.where(first, own_rows(first_out), own_rows(second_out))
    bg.add(move_task(place, out_rows, transposed, hidden_out))
    bg.step((), 3)
    bg.drain()

    def done(name, columns):
        return finish(place, stores[name][0], shards[name].shape, columns)

    (down,) = done("down", [shards["down"].shape[1]])
    (up,) = done("up", [units])
    (gate,) = done("gate", [units])
    query, key, value, out = done("attn", [width] * 4)
    mine, total = sums
    model = total.shape[1] // 2
    return (
        hidden_out[0][None, :, None],
        grad_in[0].astype(F32)[None, :, None],
        query[None],
        key[None],
        value[None],
        out.T[None],
        mine[:, :width],
        total[:, :model],
        up[None],
        gate[None],
        down[None],
        mine[:, width : width + units],
        mine[:, width + units :],
        total[:, model:],
    )


def solution(mesh):
    rows = P(None, "dp", "tensor", None)
    columns = P("section", None, "tensor")
    units = P("section", "tensor", None)
    split = P("section", "tensor")
    whole = P("section", None)
    placed = P("section", None, "dp", "tensor", None)
    weights = (columns, columns, columns, units, split, whole, columns, columns, units)
    scales = (split, split, whole)
    return jax.shard_map(
        functools.partial(body, Place(mesh)),
        mesh=mesh,
        in_specs=(rows, rows) + weights + scales,
        out_specs=(placed, placed) + weights + scales,
        check_vma=False,
    )
```

```python
import functools

import jax
import jax.numpy as jnp
from jax import lax
from jax.experimental import pallas as pl
from jax.experimental.pallas import tpu as pltpu
from jax.sharding import PartitionSpec as P

HD = 64
EPS = 1e-06
AXES = ("section", "tensor", "dp")
F32 = jnp.float32
LOW = jnp.bfloat16
VMEM_LIMIT = 24 * 1024 * 1024
BAND = 256


def cost(flops, bytes_accessed, transcendentals):
    return pl.CostEstimate(flops=0, bytes_accessed=0, transcendentals=0)


class Place:
    def __init__(self, mesh):
        self.sections = mesh.shape["section"]
        self.tensors = mesh.shape["tensor"]
        self.replicas = mesh.shape["dp"]
        self.lanes = self.tensors // 2
        self.pairs = self.replicas // 2
        self.lane_bits = [1 << bit for bit in range(self.lanes.bit_length() - 1)]
        self.pair_bits = [1 << bit for bit in range(self.pairs.bit_length() - 1)]

    def here(self):
        tensor = lax.axis_index("tensor")
        replica = lax.axis_index("dp")
        self.section = lax.axis_index("section")
        self.half = tensor // self.lanes
        self.lane = tensor % self.lanes
        self.pair = replica // 2
        self.core = replica % 2
        self.own = self.half == self.core
        self.first = self.section == 0

    def move(self, value, target):
        def index(section, half, lane, pair, core):
            tensor = half * self.lanes + lane
            return (section * self.tensors + tensor) * self.replicas + pair * 2 + core

        links = []
        for section in range(self.sections):
            for half in range(2):
                for lane in range(self.lanes):
                    for pair in range(self.pairs):
                        for core in range(2):
                            source = (section, half, lane, pair, core)
                            sink = target(*source)
                            if sink is not None:
                                links.append((index(*source), index(*sink)))
        return lax.ppermute(value, AXES, links)

    def across_cores(self, value):
        return self.move(value, lambda s, h, l, p, c: (s, h, l, p, 1 - c))

    def across_lanes(self, value, bit):
        return self.move(value, lambda s, h, l, p, c: (s, h, l ^ bit, p, c))


def to_section(s, h, l, p, c):
    return (1 - s, h, l, p, c)


def to_core(s, h, l, p, c):
    return (s, h, l, p, 1 - c)


def to_half(s, h, l, p, c):
    return (s, 1 - h, l, p, c)


def transposed(s, h, l, p, c):
    return (s, c, l, p, h) if h != c else None


def to_pair(bit):
    return lambda s, h, l, p, c: (s, h, l, p ^ bit, c)


def to_lane(bit):
    return lambda s, h, l, p, c: (s, h, l ^ bit, p, c)


def only(target, test):
    return lambda s, h, l, p, c: target(s, h, l, p, c) if test(s, h, c) else None


class Background:
    def __init__(self, place):
        self.place = place
        self.waiting = []
        self.active = []

    def add(self, task):
        self.waiting.append(task)

    def busy(self):
        return bool(self.waiting or self.active)

    def step(self, anchor, starts=1):
        if not self.busy():
            return anchor
        due = [entry for entry in self.active if entry[2] <= 1]
        kept = [(task, flying, left - 1) for task, flying, left in self.active if left > 1]
        anchor, landed = lax.optimization_barrier((anchor, [flying for _, flying, _ in due]))
        tasks = [(task, arrived) for (task, _, _), arrived in zip(due, landed)]
        for _ in range(starts):
            if self.waiting:
                tasks.append((self.waiting.pop(0), None))
        asked = []
        for task, arrived in tasks:
            try:
                wanted = task.send(arrived)
            except StopIteration:
                continue
            wanted, steps = wanted if isinstance(wanted, tuple) else (wanted, 1)
            asked.append((task, wanted, steps))
        arrays = [[array for array, _ in wanted] for _, wanted, _ in asked]
        anchor, arrays = lax.optimization_barrier((anchor, arrays))
        self.active = kept + [
            (
                task,
                [self.place.move(array, target) for array, (_, target) in zip(ready, wanted)],
                steps,
            )
            for (task, wanted, steps), ready in zip(asked, arrays)
        ]
        return anchor

    def drain(self):
        while self.busy():
            self.step((), 8)


def spec(count):
    return [pl.BlockSpec(memory_space=pltpu.VMEM)] * count


def mean_of(values):
    return jnp.mean(values, axis=-1, keepdims=True)


def row_specs(lanes, rows, width):
    part = rows // lanes
    size = min(128, part)
    per = part // size

    def spec_of(bit):
        if bit == 0:
            return pl.BlockSpec((size, width), lambda i: (i, 0))
        return pl.BlockSpec(
            (size, width), lambda i: (((i // per) ^ bit) * per + lax.rem(i, per), 0)
        )

    return rows // size, size, spec_of


def load_terms(refs):
    total = refs[0][...].astype(F32)
    for ref in refs[1:]:
        total = total + ref[...].astype(F32)
    return total


def blend_forward(lanes, hidden, branch, rate, out_dtypes):
    rows, width = hidden.shape
    branch, swaps = zip(*branch)
    steps, size, spec_of = row_specs(lanes, rows, width)

    def kernel(*refs):
        hidden_ref, rate_ref = refs[:2]
        out_refs = refs[2 + len(branch) :]
        h = hidden_ref[...].astype(F32)
        b = load_terms(refs[2 : 2 + len(branch)])
        mixed = b * lax.rsqrt(mean_of(b * b) + EPS)
        u = h + rate_ref[...] * (mixed - h)
        y = u * lax.rsqrt(mean_of(u * u) + EPS)
        for ref in out_refs:
            ref[...] = y.astype(ref.dtype)

    return pl.pallas_call(
        kernel,
        grid=(steps,),
        out_shape=[jax.ShapeDtypeStruct((rows, width), kind) for kind in out_dtypes],
        in_specs=[spec_of(0), pl.BlockSpec((1, width), lambda i: (0, 0))]
        + [spec_of(bit) for bit in swaps],
        out_specs=[spec_of(0)] * len(out_dtypes),
        compiler_params=pltpu.CompilerParams(vmem_limit_bytes=VMEM_LIMIT),
        cost_estimate=cost(
            flops=12 * rows * width, bytes_accessed=10 * rows * width, transcendentals=0
        ),
        name="blend_forward",
    )(hidden, rate, *branch)


def blend_backward(lanes, hidden, branch, rate, grads):
    rows, width = hidden.shape
    branch, branch_swaps = zip(*branch)
    grads, grad_swaps = zip(*grads)
    branches = len(branch)
    steps, size, spec_of = row_specs(lanes, rows, width)

    def kernel(*refs):
        hidden_ref, rate_ref = refs[:2]
        hidden_out, branch_out, rate_out = refs[-3:]
        h = hidden_ref[...].astype(F32)
        b = load_terms(refs[2 : 2 + branches])
        g = load_terms(refs[2 + branches : -3])
        a = rate_ref[...]
        root_b = lax.rsqrt(mean_of(b * b) + EPS)
        delta = b * root_b - h
        u = h + a * delta
        root_u = lax.rsqrt(mean_of(u * u) + EPS)
        grad_u = root_u * g - u * (root_u * root_u * root_u * mean_of(u * g))
        grad_mixed = grad_u * a
        hidden_out[...] = grad_u - grad_mixed
        rate_sum = jnp.sum(grad_u * delta, axis=0, keepdims=True)

        @pl.when(pl.program_id(0) == 0)
        def _():
            rate_out[...] = rate_sum

        @pl.when(pl.program_id(0) > 0)
        def _():
            rate_out[...] += rate_sum

        grad_b = root_b * grad_mixed - b * (
            root_b * root_b * root_b * mean_of(b * grad_mixed)
        )
        branch_out[...] = grad_b.astype(branch_out.dtype)

    one_row = pl.BlockSpec((1, width), lambda i: (0, 0))
    return pl.pallas_call(
        kernel,
        grid=(steps,),
        out_shape=[
            jax.ShapeDtypeStruct((rows, width), F32),
            jax.ShapeDtypeStruct((rows, width), LOW),
            jax.ShapeDtypeStruct((1, width), F32),
        ],
        in_specs=[spec_of(0), one_row] + [spec_of(bit) for bit in branch_swaps + grad_swaps],
        out_specs=[spec_of(0), spec_of(0), one_row],
        compiler_params=pltpu.CompilerParams(
            vmem_limit_bytes=VMEM_LIMIT, dimension_semantics=("arbitrary",)
        ),
        cost_estimate=cost(
            flops=30 * rows * width, bytes_accessed=20 * rows * width, transcendentals=0
        ),
        name="blend_backward",
    )(hidden, rate, *branch, *grads)


def head_masks(width):
    lanes = lax.broadcasted_iota(jnp.int32, (1, width), 1)
    return [
        (lanes >= head * HD) & (lanes < (head + 1) * HD) for head in range(width // HD)
    ]


def head_mean(values, masks):
    if len(masks) == 1:
        return jnp.sum(values, axis=-1, keepdims=True) * (1.0 / HD)
    result = None
    for mask in masks:
        total = jnp.sum(jnp.where(mask, values, 0.0), axis=-1, keepdims=True) * (1.0 / HD)
        result = total if result is None else jnp.where(mask, total, result)
    return result


def nt_dot(left, right):
    return lax.dot_general(left, right, (((1,), (1,)), ((), ())), preferred_element_type=F32)


def tn_dot(left, right):
    return lax.dot_general(left, right, (((0,), (0,)), ((), ())), preferred_element_type=F32)


def nn_dot(left, right):
    return lax.dot_general(left, right, (((1,), (0,)), ((), ())), preferred_element_type=F32)


def fused_dot(xs, used, tiled, outs, epilogue, tile, name, keep=None, at=0, count=1, total=None):
    rows = sum(piece.shape[0] for piece in xs[0])
    outer = used[0][3][0] if len(used[0]) > 3 else used[0][1].shape[0 if used[0][2] else 1]
    tile = min(tile, outer)
    steps = outer // tile
    operands, in_specs = [], []

    def whole(array):
        operands.append(array)
        in_specs.append(pl.BlockSpec(array.shape, lambda i: (0, 0)))

    for pieces in xs:
        for piece in pieces:
            whole(piece)
    for _, weight, flipped, *place in used:
        operands.append(weight)
        begin = place[0][1] if place else 0
        if flipped:
            in_specs.append(pl.BlockSpec((tile, weight.shape[1]), lambda i: (i, 0)))
        else:
            in_specs.append(
                pl.BlockSpec((weight.shape[0], tile), lambda i, begin=begin: (0, begin + i))
            )
    for array, stacked in tiled:
        operands.append(array)
        if stacked:
            in_specs.append(pl.BlockSpec((rows, tile), lambda i: (at, i)))
        else:
            in_specs.append(pl.BlockSpec((array.shape[0], tile), lambda i: (0, i)))
    total_weights = total[0] if total else []
    for weight, flipped in total_weights:
        operands.append(weight)
        if flipped:
            in_specs.append(pl.BlockSpec((weight.shape[0], tile), lambda i: (0, i)))
        else:
            in_specs.append(pl.BlockSpec((tile, weight.shape[1]), lambda i: (i, 0)))
    out_shape, out_specs, aliases, behind = [], [], {}, []

    def stacked_out(kind, columns, block, index, stack):
        if stack:
            aliases[len(operands) + len(behind)] = len(out_shape)
            behind.append(stack[-1])
        out_shape.append(jax.ShapeDtypeStruct((rows * count, columns), kind))
        out_specs.append(pl.BlockSpec(block, index))

    for out_rows, kind, stack in outs:
        if stack is None:
            out_shape.append(jax.ShapeDtypeStruct((out_rows, outer), kind))
            out_specs.append(pl.BlockSpec((out_rows, tile), lambda i: (0, i)))
        else:
            stacked_out(kind, outer, (rows, tile), lambda i: (at, i), stack)
    inner = xs[0][0].shape[1]
    if keep is not None:
        stacked_out(LOW, inner, (rows, inner), lambda i: (at, 0), keep)
    pieces_out = 0
    scratch = []
    if total:
        weight, flipped = total_weights[0]
        columns = weight.shape[0 if flipped else 1]
        pieces_out = 2
        for _ in range(2):
            out_shape.append(jax.ShapeDtypeStruct((rows // 2, columns), LOW))
            out_specs.append(pl.BlockSpec((rows // 2, columns), lambda i: (0, 0)))
        scratch.append(pltpu.VMEM((rows, columns), F32))
    counts = [len(pieces) for pieces in xs]

    def kernel(*refs):
        refs = list(refs)

        def take(number):
            taken, refs[:number] = refs[:number], []
            return taken

        x_refs = [take(number) for number in counts]
        weight_refs = take(len(used))
        tiled_refs = take(len(tiled))
        total_refs = take(len(total_weights))
        take(len(behind))
        out_refs = take(len(outs))
        keep_ref = take(1)[0] if keep is not None else None
        piece_refs = take(pieces_out)
        step = pl.program_id(0)
        if keep_ref is not None:

            @pl.when(step == 0)
            def _():
                start = 0
                for ref in x_refs[0]:
                    keep_ref[start : start + ref.shape[0], :] = ref[...]
                    start += ref.shape[0]

        values = [keep_ref if at_x == 0 and keep_ref is not None else members[0]
                  for at_x, members in enumerate(x_refs)]
        sums = [None] * len(outs)
        band = min(BAND, rows)
        for begin in range(0, rows, band):
            here = slice(begin, begin + band)
            dots = [
                (nt_dot if flipped else nn_dot)(values[which][here, :], ref[...])
                for (which, _, flipped, *_), ref in zip(used, weight_refs)
            ]
            results, terms = epilogue(
                dots, [ref[here, :] if ref.shape[0] == rows else ref[...] for ref in tiled_refs]
            )
            for at_out, (ref, result) in enumerate(zip(out_refs, results)):
                if ref.shape[0] == rows:
                    ref[here, :] = result.astype(ref.dtype)
                else:
                    former = sums[at_out]
                    sums[at_out] = result if former is None else former + result
            if total:
                sum_ref = refs[0]
                term = None
                for (_, flipped), ref, value in zip(total_weights, total_refs, terms):
                    product = (nt_dot if flipped else nn_dot)(value, ref[...])
                    term = product if term is None else term + product
                sum_ref[here, :] = jnp.where(step == 0, 0.0, sum_ref[here, :]) + term
        for ref, result in zip(out_refs, sums):
            if result is not None:
                ref[...] = result.astype(ref.dtype)
        if total:

            @pl.when(step == steps - 1)
            def _():
                start = 0
                for ref in piece_refs:
                    ref[...] = sum_ref[start : start + ref.shape[0], :].astype(LOW)
                    start += ref.shape[0]

    flops = sum(2 * rows * weight.shape[0] * weight.shape[1] for _, weight, *_ in used)
    flops += sum(2 * rows * weight.shape[0] * weight.shape[1] for weight, _ in total_weights)
    moved = sum(array.size * array.dtype.itemsize for array in operands)
    results = pl.pallas_call(
        kernel,
        grid=(steps,),
        out_shape=out_shape,
        in_specs=in_specs + [pl.BlockSpec(memory_space=pl.ANY)] * len(behind),
        out_specs=out_specs,
        scratch_shapes=scratch,
        input_output_aliases=aliases,
        compiler_params=pltpu.CompilerParams(
            vmem_limit_bytes=VMEM_LIMIT, dimension_semantics=("arbitrary",)
        ),
        cost_estimate=cost(flops=flops, bytes_accessed=2 * moved, transcendentals=0),
        name=name,
    )(*operands, *behind)
    results = list(results)
    for (_, _, stack), result in zip(outs, results):
        if stack is not None:
            stack.append(result)
    if keep is not None:
        keep.append(results[len(outs)])
    return results[: len(outs)], results[len(results) - pieces_out :]


def project(pieces, packed, width, at, count, keep):
    rows = sum(piece.shape[0] for piece in pieces)
    used = 3 * width if width % 128 == 0 else 4 * width
    results, _ = fused_dot(
        [pieces],
        [(0, packed, False, (used, 0))],
        [],
        [(rows, F32, None)],
        lambda dots, _: (dots, None),
        width if width % 128 == 0 else used,
        "project",
        keep=keep,
        at=at,
        count=count,
    )
    return results[0]


def sigmoid_of(values):
    return 0.5 + 0.5 * jnp.tanh(0.5 * values)


def mlp_forward(pieces, weights, scales, at, count, stacks):
    up_w, gate_w, down_w = weights
    rows = sum(piece.shape[0] for piece in pieces)

    def epilogue(dots, tiles):
        up_raw, gate_raw = dots
        up_scale, gate_scale = tiles
        gated = gate_raw * gate_scale
        inner = (gated * sigmoid_of(gated) * (up_raw * up_scale)).astype(LOW)
        return [up_raw, gate_raw, inner], [inner]

    mid, up_raw, gate_raw, inner = stacks
    _, out = fused_dot(
        [pieces],
        [(0, up_w, False), (0, gate_w, False)],
        [(scales[0], False), (scales[1], False)],
        [(rows, LOW, up_raw), (rows, LOW, gate_raw), (rows, LOW, inner)],
        epilogue,
        256,
        "mlp_forward",
        keep=mid,
        at=at,
        count=count,
        total=([(down_w, False)], None),
    )
    return out


def mlp_backward(pieces, weights, scales, raws, at, count, stacks):
    up_w, gate_w, down_w = weights
    rows = sum(piece.shape[0] for piece in pieces)

    def epilogue(dots, tiles):
        up_raw, gate_raw, up_scale, gate_scale = tiles
        up_raw, gate_raw = up_raw.astype(F32), gate_raw.astype(F32)
        grad = dots[0]
        gated = gate_raw * gate_scale
        sigmoid = sigmoid_of(gated)
        silu = gated * sigmoid
        slope = sigmoid * (1.0 + gated * (1.0 - sigmoid))
        from_up = grad * silu
        from_gate = grad * (up_raw * up_scale) * slope
        up_back = (from_up * up_scale).astype(LOW)
        gate_back = (from_gate * gate_scale).astype(LOW)
        up_sum = jnp.sum(from_up * up_raw, axis=0, keepdims=True)
        gate_sum = jnp.sum(from_gate * gate_raw, axis=0, keepdims=True)
        return [up_back, gate_back, up_sum, gate_sum], [up_back, gate_back]

    full, up_back, gate_back = stacks
    results, out = fused_dot(
        [pieces],
        [(0, down_w, True)],
        [(raws[0], True), (raws[1], True), (scales[0], False), (scales[1], False)],
        [(rows, LOW, up_back), (rows, LOW, gate_back), (1, F32, None), (1, F32, None)],
        epilogue,
        256,
        "mlp_backward",
        keep=full,
        at=at,
        count=count,
        total=([(up_w, True), (gate_w, True)], None),
    )
    return results[2], results[3], out


def output_backward(pieces, output_w, at, count, keep):
    rows = sum(piece.shape[0] for piece in pieces)
    results, _ = fused_dot(
        [pieces],
        [(0, output_w, True)],
        [],
        [(rows, LOW, None)],
        lambda dots, _: (dots, None),
        256,
        "output_backward",
        keep=keep,
        at=at,
        count=count,
    )
    return results[0]


def block_starts(places_ref, blocks, part):
    return [
        (block, pl.multiple_of(places_ref[block] * part, part)) for block in range(blocks)
    ]


def load_heads(starts, part, width, gain, masks, raw_ref, query, key, value):
    for block, start in starts:
        rows = pl.ds(block * part, part)
        place = pl.ds(start, part)
        raw = raw_ref[rows, 0:width]
        root = lax.rsqrt(head_mean(raw * raw, masks) + EPS)
        query[place, :] = (raw * root * gain).astype(LOW) * LOW(HD ** (-0.5))
        raw = raw_ref[rows, width : 2 * width]
        root = lax.rsqrt(head_mean(raw * raw, masks) + EPS)
        key[place, :] = (raw * root * gain).astype(LOW)
        value[place, :] = raw_ref[rows, 2 * width : 3 * width].astype(LOW)


def whole_spec(array):
    return pl.BlockSpec(array.shape, lambda i: (0, 0))


def stacked_specs(stack, operands):
    if not stack:
        return [], [], {}
    return [stack[-1]], [pl.BlockSpec(memory_space=pl.ANY)], {operands: 0}


def attention_forward(places, scale, raw, output_w, at, count, stack):
    width = scale.shape[1]
    blocks = places.shape[0]
    length = raw.shape[0]
    part = length // blocks
    span = min(256, length)
    model = output_w.shape[1]
    behind, behind_specs, aliases = stacked_specs(stack, 4)

    def kernel(*refs):
        places_ref, scale_ref, output_ref, raw_ref = refs[:4]
        attended_ref, mine_ref, theirs_ref, query, key, value, result = refs[4 + len(behind) :]
        masks = head_masks(width)
        starts = block_starts(places_ref, blocks, part)
        load_heads(starts, part, width, scale_ref[...], masks, raw_ref, query, key, value)
        row_at = lax.broadcasted_iota(jnp.int32, (span, span), 0)
        col_at = lax.broadcasted_iota(jnp.int32, (span, span), 1)
        causal = col_at <= row_at
        for begin in range(0, length, span):
            rows = query[begin : begin + span, :]
            total = None
            for mask in masks:
                picked = jnp.where(mask, rows, LOW(0))
                last = nt_dot(picked, key[begin : begin + span, :])
                last = jnp.where(causal, jnp.exp(last), 0.0)
                weight = jnp.sum(last, axis=-1, keepdims=True)
                head = nn_dot(last.astype(LOW), value[begin : begin + span, :])
                if begin > 0:
                    first = jnp.exp(nt_dot(picked, key[0:begin, :]))
                    weight = weight + jnp.sum(first, axis=-1, keepdims=True)
                    head = head + nn_dot(first.astype(LOW), value[0:begin, :])
                head = head * (1.0 / weight)
                total = head if total is None else jnp.where(mask, head, total)
            result[begin : begin + span, :] = total.astype(LOW)
        for block, start in starts:
            attended_ref[block * part : (block + 1) * part, :] = result[pl.ds(start, part), :]
        half = length // 2
        mine_ref[...] = nn_dot(attended_ref[:half, :], output_ref[...]).astype(LOW)
        theirs_ref[...] = nn_dot(attended_ref[half:, :], output_ref[...]).astype(LOW)

    attended, mine, theirs = pl.pallas_call(
        kernel,
        grid=(1,),
        out_shape=[
            jax.ShapeDtypeStruct((length * count, width), LOW),
            jax.ShapeDtypeStruct((length // 2, model), LOW),
            jax.ShapeDtypeStruct((length // 2, model), LOW),
        ],
        in_specs=[pl.BlockSpec(memory_space=pltpu.SMEM)]
        + [whole_spec(array) for array in (scale, output_w, raw)]
        + behind_specs,
        out_specs=[pl.BlockSpec((length, width), lambda i: (at, 0))]
        + [pl.BlockSpec((length // 2, model), lambda i: (0, 0))] * 2,
        scratch_shapes=[pltpu.VMEM((length, width), LOW)] * 4,
        input_output_aliases=aliases,
        compiler_params=pltpu.CompilerParams(vmem_limit_bytes=VMEM_LIMIT),
        cost_estimate=cost(
            flops=8 * length * length * width,
            bytes_accessed=24 * length * width,
            transcendentals=length * length * (width // HD),
        ),
        name="attention_forward",
    )(places, scale, output_w, raw, *behind)
    stack.append(attended)
    return mine, theirs


def attention_backward(places, scale, raw, grads, packed, at, count, stack):
    width = scale.shape[1]
    blocks = places.shape[0]
    length = raw.shape[0]
    part = length // blocks
    span = min(256, length)
    model = packed.shape[0]
    behind, behind_specs, aliases = stacked_specs(stack, 5)

    def kernel(*refs):
        places_ref, scale_ref, packed_ref, raw_ref, grad_ref = refs[:5]
        back_ref, scale_out, mine_ref, theirs_ref = refs[5 + len(behind) : 9 + len(behind)]
        query, key, value, grad, query_sum, key_sum, value_sum = refs[9 + len(behind) :]
        masks = head_masks(width)
        gain = scale_ref[...]
        starts = block_starts(places_ref, blocks, part)
        load_heads(starts, part, width, gain, masks, raw_ref, query, key, value)
        for block, start in starts:
            grad[pl.ds(start, part), :] = grad_ref[block * part : (block + 1) * part, :]
        key_sum[...] = jnp.zeros_like(key_sum)
        value_sum[...] = jnp.zeros_like(value_sum)
        key_at = lax.broadcasted_iota(jnp.int32, (span, span), 0)
        query_at = lax.broadcasted_iota(jnp.int32, (span, span), 1)
        causal = key_at <= query_at
        for origin in range(0, length, span):
            rows = query[origin : origin + span, :]
            grad_rows = grad[origin : origin + span, :]
            total = None
            for mask in masks:
                picked = jnp.where(mask, rows, LOW(0))
                grad_picked = jnp.where(mask, grad_rows, LOW(0))
                pieces = [slice(0, origin)] if origin > 0 else []
                pieces.append(slice(origin, origin + span))
                raised = [jnp.exp(nt_dot(key[piece, :], picked)) for piece in pieces]
                raised[-1] = jnp.where(causal, raised[-1], 0.0)
                weight = sum(jnp.sum(member, axis=0, keepdims=True) for member in raised)
                inverse = 1.0 / weight
                probs = [member * inverse for member in raised]
                grad_probs = [nt_dot(value[piece, :], grad_picked) for piece in pieces]
                row_sum = sum(
                    jnp.sum(left * right, axis=0, keepdims=True)
                    for left, right in zip(probs, grad_probs)
                )
                head = None
                for piece, prob, grad_prob in zip(pieces, probs, grad_probs):
                    grad_score = (prob * (grad_prob - row_sum)).astype(LOW)
                    value_sum[piece, :] += nn_dot(prob.astype(LOW), grad_picked)
                    key_sum[piece, :] += nn_dot(grad_score, picked)
                    term = tn_dot(grad_score, key[piece, :])
                    head = term if head is None else head + term
                total = head if total is None else jnp.where(mask, head, total)
            query_sum[origin : origin + span, :] = total * (HD ** (-0.5))
        scale_sum = jnp.zeros((1, width), F32)
        for block, start in starts:
            rows = slice(block * part, (block + 1) * part)
            place = pl.ds(start, part)
            for slot, source in ((0, query_sum), (1, key_sum)):
                lanes = slice(slot * width, (slot + 1) * width)
                raw_rows = raw_ref[rows, lanes]
                root = lax.rsqrt(head_mean(raw_rows * raw_rows, masks) + EPS)
                grad_low = source[place, :]
                scale_sum = scale_sum + jnp.sum(
                    grad_low * (raw_rows * root), axis=0, keepdims=True
                )
                grad_unit = grad_low * gain
                cross = head_mean(raw_rows * grad_unit, masks)
                result = root * grad_unit - raw_rows * (root * root * root * cross)
                back_ref[rows, lanes] = result.astype(LOW)
            back_ref[rows, 2 * width : 3 * width] = value_sum[place, :].astype(LOW)
        scale_out[...] = scale_sum
        half = length // 2
        weights = packed_ref[:, : 3 * width]
        mine_ref[...] = nt_dot(back_ref[:half, :], weights).astype(LOW)
        theirs_ref[...] = nt_dot(back_ref[half:, :], weights).astype(LOW)

    back, scale_sum, mine, theirs = pl.pallas_call(
        kernel,
        grid=(1,),
        out_shape=[
            jax.ShapeDtypeStruct((length * count, 3 * width), LOW),
            jax.ShapeDtypeStruct((1, width), F32),
            jax.ShapeDtypeStruct((length // 2, model), LOW),
            jax.ShapeDtypeStruct((length // 2, model), LOW),
        ],
        in_specs=[pl.BlockSpec(memory_space=pltpu.SMEM)]
        + [whole_spec(array) for array in (scale, packed, raw, grads)]
        + behind_specs,
        out_specs=[
            pl.BlockSpec((length, 3 * width), lambda i: (at, 0)),
            pl.BlockSpec((1, width), lambda i: (0, 0)),
        ]
        + [pl.BlockSpec((length // 2, model), lambda i: (0, 0))] * 2,
        scratch_shapes=[pltpu.VMEM((length, width), LOW)] * 4
        + [pltpu.VMEM((length, width), F32)] * 3,
        input_output_aliases=aliases,
        compiler_params=pltpu.CompilerParams(vmem_limit_bytes=VMEM_LIMIT),
        cost_estimate=cost(
            flops=20 * length * length * width,
            bytes_accessed=32 * length * width,
            transcendentals=length * length * (width // HD),
        ),
        name="attention_backward",
    )(places, scale, packed, raw, grads, *behind)
    stack.append(back)
    return scale_sum, mine, theirs


def gather(place, value):
    half = value.shape[0] // 2
    return [value, place.across_cores(value[:half]), place.across_cores(value[half:])]


def gather_lanes(place, value):
    rows = [value]
    for bit in place.lane_bits:
        rows = rows + [place.across_lanes(member, bit) for member in rows]
    return jnp.concatenate(rows, axis=0)


def exchange(place, total):
    terms = [(total, 0)]
    for bit in place.lane_bits:
        total = terms[0][0]
        for value, swapped in terms[1:]:
            total = plus(total, unswapped(place, value, swapped))
        terms = [(total, 0), (place.across_lanes(total, bit), bit)]
    return terms


def unswapped(place, value, bit):
    part = value.shape[0] // place.lanes
    order = [value[(at ^ bit) * part : ((at ^ bit) + 1) * part] for at in range(place.lanes)]
    return jnp.concatenate(order, axis=0)


def spread_task(place, name, shard, steps, ready):
    rows = shard.shape[0] // place.pairs
    cut = lax.dynamic_slice_in_dim(shard, place.pair * rows, rows, 0)
    parts = yield [(cut, only(to_half, lambda s, h, c: c == h))], steps
    for bit in place.pair_bits:
        got = yield [(part, only(to_pair(bit), lambda s, h, c: c != h)) for part in parts]
        parts = parts + got
    ready[name] = assemble(place, shard, parts)


def assemble(place, shard, parts):
    pairs = place.pairs
    flags = jnp.stack([place.own.astype(jnp.int32), place.pair])

    def kernel(flags_ref, own_ref, *refs):
        part_refs, out_ref, sems = refs[:pairs], refs[pairs], refs[-1]

        @pl.when(flags_ref[0] == 1)
        def _():
            copy = pltpu.make_async_copy(own_ref, out_ref, sems.at[0])
            copy.start()
            copy.wait()

        @pl.when(flags_ref[0] == 0)
        def _():
            copies = []
            for step in range(pairs):
                rows = part_refs[step].shape[0]
                begin = pl.multiple_of((flags_ref[1] ^ step) * rows, rows)
                sink = out_ref.at[pl.ds(begin, rows), :]
                copies.append(pltpu.make_async_copy(part_refs[step], sink, sems.at[step]))
            for copy in copies:
                copy.start()
            for copy in copies:
                copy.wait()

    return pl.pallas_call(
        kernel,
        out_shape=jax.ShapeDtypeStruct(shard.shape, shard.dtype),
        in_specs=[pl.BlockSpec(memory_space=pltpu.SMEM)]
        + [pl.BlockSpec(memory_space=pl.ANY)] * (1 + pairs),
        out_specs=pl.BlockSpec(memory_space=pltpu.VMEM),
        scratch_shapes=[pltpu.SemaphoreType.DMA((pairs,))],
        compiler_params=pltpu.CompilerParams(vmem_limit_bytes=VMEM_LIMIT),
        cost_estimate=cost(
            flops=0, bytes_accessed=4 * shard.size, transcendentals=0
        ),
        name="assemble",
    )(flags, shard, *parts)


def halved(value, bit, rows):
    half = rows // 2
    kept = lax.dynamic_slice_in_dim(value, bit * half, half, 0)
    sent = lax.dynamic_slice_in_dim(value, (1 - bit) * half, half, 0)
    return kept, sent


def plus(left, right):
    return (left.astype(F32) + right.astype(F32)).astype(LOW)


def collect_task(place, grad, store, steps):
    held = grad
    for bit in place.pair_bits[::-1]:
        kept, sent = halved(held, (place.pair // bit) % 2, held.shape[0])
        (met,) = yield [(sent, to_pair(bit))], steps[0]
        held = plus(kept, met)
    (met,) = yield [(held, only(to_half, lambda s, h, c: c != h))], steps[1]
    held = plus(held, met)
    parts = [held]
    for bit in place.pair_bits:
        got = yield [(value, only(to_pair(bit), lambda s, h, c: c == h)) for value in parts]
        parts = parts + got
    got = yield [(value, only(to_core, lambda s, h, c: c == h)) for value in parts]
    store.append((parts, got))


def finish(place, sides, shape, columns):
    pairs = place.pairs
    rows, width = shape
    piece = rows // pairs
    flags = jnp.stack([place.own.astype(jnp.int32), place.pair])
    operands = [member for side in sides for member in side]

    def kernel(flags_ref, *refs):
        part_refs = refs[: len(operands)]
        out_refs = refs[len(operands) : -2]
        landing, sems = refs[-2:]
        step = pl.program_id(0)

        @pl.when(step == 0)
        def _():
            for side in range(2):

                @pl.when(flags_ref[0] == 1 - side)
                def _():
                    for relative in range(pairs):
                        block = flags_ref[1] ^ relative
                        pltpu.make_async_copy(
                            part_refs[side * pairs + relative],
                            landing.at[block],
                            sems.at[block],
                        ).start()

        pltpu.make_async_copy(part_refs[0], landing.at[step], sems.at[step]).wait()
        value = landing[step].astype(F32)
        begin = 0
        for count, ref in zip(columns, out_refs):
            ref[...] = value[:, begin : begin + count]
            begin += count

    return pl.pallas_call(
        kernel,
        grid=(pairs,),
        out_shape=[jax.ShapeDtypeStruct((rows, count), F32) for count in columns],
        in_specs=[pl.BlockSpec(memory_space=pltpu.SMEM)]
        + [pl.BlockSpec(memory_space=pl.ANY)] * len(operands),
        out_specs=[pl.BlockSpec((piece, count), lambda i: (i, 0)) for count in columns],
        scratch_shapes=[
            pltpu.VMEM((pairs, piece, width), LOW),
            pltpu.SemaphoreType.DMA((pairs,)),
        ],
        compiler_params=pltpu.CompilerParams(
            vmem_limit_bytes=VMEM_LIMIT, dimension_semantics=("arbitrary",)
        ),
        cost_estimate=cost(
            flops=0, bytes_accessed=6 * rows * width, transcendentals=0
        ),
        name="finish",
    )(flags, *operands)


def move_task(place, value, target, store, steps=1):
    (met,) = yield [(value, target)], steps
    store.append(jnp.where(place.own, value, met))


def small_task(place, small, rates, store):
    count = small.shape[1]
    slots = jnp.concatenate(
        [jnp.where(place.core == slot, small, 0.0) for slot in range(2)] + [rates], axis=1
    )
    targets = [to_core, to_half] + [to_pair(bit) for bit in place.pair_bits]
    for target in targets:
        (met,) = yield [(slots, target)]
        slots = slots + met
    store.append(jnp.where(place.half == 0, slots[:, :count], slots[:, count : 2 * count]))
    store.append(slots[:, 2 * count :])


class Weights:
    def __init__(self, bg, width, ready):
        self.bg, self.width, self.ready = bg, width, ready

    def wait(self, names, anchor):
        while any(name not in self.ready for name in names):
            anchor = self.bg.step(anchor)
        if "out" not in self.ready:
            self.ready["out"] = self.ready["attn"][:, 3 * self.width :].T
        return anchor

    def __getitem__(self, name):
        return self.ready[name]


class Chain:
    def __init__(self, place, bg):
        self.place, self.bg = place, bg
        self.last = None
        self.ready = None
        self.beside = []

    def exchange(self, mine, theirs, starts=None):
        if starts is not None:
            theirs = self.bg.step(theirs, starts)
        last = self.last or []
        flying = [value for value, _ in last]
        theirs, flying, beside = lax.optimization_barrier((theirs, flying, self.beside))
        last[:] = [(value, bit) for value, (_, bit) in zip(flying, last)]
        self.beside[:] = beside
        self.beside = []
        self.ready = plus(mine, self.place.across_cores(theirs))
        self.last = []
        return self.last

    def after(self, values):
        if self.ready is not None:
            values, total = lax.optimization_barrier((values, self.ready))
            self.ready = None
            self.last[:] = exchange(self.place, total)
        return values

    def terms_after(self, terms):
        if terms is self.last and self.ready is not None:
            self.after([])
        values = self.after([value for value, _ in terms])
        return [(value, bit) for value, (_, bit) in zip(values, terms)]


def layer_forward(place, places, bg, chain, rows, weights, scales, late=None):
    qk_scale, attn_rate, up_scale, gate_scale, mlp_rate = scales
    width = qk_scale.shape[1]
    lanes = place.lanes
    full_in, attended, raws, attn_terms = [], [], [], []
    pieces = weights.wait(("attn",), chain.after(gather(place, rows[0])))
    if late:
        rows = rows + late()
        chain.beside = rows[1:]
    count = len(rows)
    streams = range(count)
    for at in streams:
        if at > 0:
            pieces = chain.after(gather(place, rows[at]))
        raws.append(project(pieces, weights["attn"], width, at, count, full_in))
        mine, theirs = attention_forward(
            places, qk_scale, raws[at], weights["out"], at, count, attended
        )
        attn_terms.append(chain.exchange(mine, theirs, 1))
    middles, mlp_terms = [], []
    stacks = [[], [], [], []]
    for at in streams:
        terms = chain.terms_after(attn_terms[at])
        middles.append(blend_forward(lanes, rows[at], terms, attn_rate, [F32, LOW]))
        pieces = gather(place, middles[at][1])
        pieces = weights.wait(("up", "gate", "down"), pieces)
        mine, theirs = mlp_forward(
            pieces,
            (weights["up"], weights["gate"], weights["down"]),
            (up_scale, gate_scale),
            at,
            count,
            stacks,
        )
        mlp_terms.append(chain.exchange(mine, theirs))

    def result(at, after=()):
        terms = chain.terms_after(mlp_terms[at])
        middle = middles[at][0]
        middle, after = lax.optimization_barrier((middle, after))
        return blend_forward(lanes, middle, terms, mlp_rate, [LOW])[0]

    kept = (rows, full_in[-1], raws, attended[-1], attn_terms, middles, stacks, mlp_terms)
    return result, kept


def layer_backward(place, places, bg, chain, grads, kept, weights, scales, collect, starts):
    rows, full_in, raws, attended, attn_terms, middles, stacks, mlp_terms = kept
    full_mid, up_raw, gate_raw, inner = (stack[-1] for stack in stacks)
    qk_scale, attn_rate, up_scale, gate_scale, mlp_rate = scales
    count = len(rows)
    streams = range(count)
    lanes = place.lanes

    mlp_back, sums, mid_terms = [], [], []
    back_stacks = [[], [], []]
    for at in streams:
        terms = chain.terms_after(grads[at])
        mlp_back.append(
            blend_backward(lanes, middles[at][0], mlp_terms[at], mlp_rate, terms)
        )
        pieces = gather(place, mlp_back[at][1])
        up_sum, gate_sum, (mine, theirs) = mlp_backward(
            pieces,
            (weights["up"], weights["gate"], weights["down"]),
            (up_scale, gate_scale),
            (up_raw, gate_raw),
            at,
            count,
            back_stacks,
        )
        sums.append((up_sum, gate_sum))
        mid_terms.append(chain.exchange(mine, theirs, starts["mlp"][at]))
    full_mlp, up_back, gate_back = chain.after([stack[-1] for stack in back_stacks])
    collect("down", [(inner, full_mlp)])
    collect("up", [(full_mid, up_back)])
    collect("gate", [(full_mid, gate_back)])
    attn_back, full_attn, back, in_terms, qk_sums = [], [], [], [], []
    for at in streams:
        terms = chain.terms_after([(mlp_back[at][0], 0)] + mid_terms[at])
        attn_back.append(blend_backward(lanes, rows[at], attn_terms[at], attn_rate, terms))
        pieces = gather(place, attn_back[at][1])
        if starts["attention"][at] is not None:
            pieces = bg.step(pieces, starts["attention"][at])
        grad_attended = output_backward(pieces, weights["out"], at, count, full_attn)
        qk_sum, mine, theirs = attention_backward(
            places, qk_scale, raws[at], grad_attended, weights["attn"], at, count, back
        )
        qk_sums.append(qk_sum)
        in_terms.append(chain.exchange(mine, theirs, starts["end"][at]))
    last = chain.after(back[-1])
    collect("attn", [(full_in, last), (full_attn[-1], attended)])
    small = jnp.concatenate(
        [sum(qk_sums), sum(member[0] for member in sums), sum(member[1] for member in sums)],
        axis=1,
    )
    rates = jnp.concatenate(
        [sum(member[2] for member in attn_back), sum(member[2] for member in mlp_back)], axis=1
    )
    grad_rows = [[(attn_back[at][0], 0)] + in_terms[at] for at in streams]
    return grad_rows, small, rates


def body(place, *args):
    (
        hidden_in,
        cotangent,
        query_w,
        key_w,
        value_w,
        output_w,
        qk_scale,
        attn_rate,
        up_w,
        gate_w,
        down_w,
        up_scale,
        gate_scale,
        mlp_rate,
    ) = args
    place.here()
    first = place.first
    width, units = query_w.shape[2], up_w.shape[2]
    part = hidden_in.shape[2]
    streams = range(hidden_in.shape[0])
    bg = Background(place)
    chain = Chain(place, bg)

    shards = {
        "attn": jnp.concatenate([query_w[0], key_w[0], value_w[0], output_w[0].T], axis=1),
        "up": up_w[0],
        "gate": gate_w[0],
        "down": down_w[0],
    }
    ready = {}

    small_in = jnp.concatenate([qk_scale, up_scale, gate_scale], axis=1)
    start_rows, small_rows = [], []
    start = [jnp.where(first, hidden_in[at, 0], cotangent[at, 0]) for at in streams]
    bg.add(move_task(place, start[0], transposed, start_rows))
    bg.add(move_task(place, small_in, only(to_half, lambda s, h, c: c == h), small_rows))
    bg.add(spread_task(place, "attn", shards["attn"], 1, ready))
    bg.step((), 3)
    for member in start[1:]:
        bg.add(move_task(place, member, transposed, start_rows))
    for name in ("up", "gate", "down"):
        bg.add(spread_task(place, name, shards[name], 1, ready))
    bg.step((), len(start))
    start = [gather_lanes(place, start_rows[0])]

    def late_rows():
        start.extend(gather_lanes(place, member) for member in start_rows[1:])
        return start[1:]

    edges = [0, width, width + units, width + 2 * units]
    qk, up, gate = (small_rows[0][:, a:b] for a, b in zip(edges[:3], edges[1:]))
    scales = (qk, attn_rate, up, gate, mlp_rate)
    weights = Weights(bg, width, ready)

    blocks = [
        (place.core ^ other) * place.lanes + (place.lane ^ step)
        for other in range(2)
        for step in range(place.lanes)
    ]
    places = jnp.stack(blocks).astype(jnp.int32)

    def own_rows(members):
        return jnp.stack([member[:part] for member in members])

    def hop(value, source):
        return place.move(value, only(to_section, lambda s, h, c: s == source))

    def summed(terms):
        total = terms[0][0].astype(F32)
        for value, bit in terms[1:]:
            total = total + (unswapped(place, value, bit) if bit else value).astype(F32)
        return total.astype(LOW)

    def hops(members, source):
        arrived = [hop(member, source) for member in members]
        arrived[0], members = lax.optimization_barrier((arrived[0], members))
        chain.beside = arrived
        return arrived

    result, kept_first = layer_forward(
        place, places, bg, chain, start[:1], weights, scales, late_rows
    )
    first_out = [result(at) for at in streams]
    second_in = hops(first_out, 0)
    result, kept_second = layer_forward(place, places, bg, chain, second_in, weights, scales)
    hidden_out, grad_in, sums = [], [], []
    late = {}
    none = [None] * len(streams)
    grad_mid, second_small, second_rates = layer_backward(
        place,
        places,
        bg,
        chain,
        [[(member, 0)] for member in start],
        kept_second,
        weights,
        scales,
        late.__setitem__,
        {"mlp": none, "attention": none, "end": none},
    )

    def product(factors):
        parts = [tn_dot(left, right) for left, right in factors]
        return (parts[0] if len(parts) == 1 else jnp.concatenate(parts, axis=1)).astype(LOW)

    grad_second = [summed(terms) for terms in grad_mid]
    late, grad_second[0] = lax.optimization_barrier((late, grad_second[0]))
    late = {name: product(factors) for name, factors in late.items()}
    second_out = [result(at, grad_second[0]) for at in streams]
    out_rows = jnp.where(first, own_rows(first_out), own_rows(second_out))
    grad_back = hops(grad_second, 1)
    grad_back[0], late, out_rows = lax.optimization_barrier((grad_back[0], late, out_rows))
    stores = {name: [] for name in shards}

    def collect(name, factors):
        mine = jnp.where(first, product(factors), late[name])
        bg.add(collect_task(place, mine, stores[name], (1, 1)))
        if name == "down":
            bg.add(move_task(place, out_rows, transposed, hidden_out))

    grad_start, first_small, first_rates = layer_backward(
        place,
        places,
        bg,
        chain,
        [[(member, 0)] for member in grad_back],
        kept_first,
        weights,
        scales,
        collect,
        {
            "mlp": none,
            "attention": [2] + [1] * (len(streams) - 1),
            "end": [1] + [0] * (len(streams) - 1),
        },
    )
    bg.add(
        small_task(
            place,
            jnp.where(first, first_small, second_small),
            jnp.where(first, first_rates, second_rates),
            sums,
        )
    )

    def in_rows(at):
        value = jnp.where(first, summed(grad_start[at])[:part], grad_second[at][:part])
        return move_task(place, value, transposed, grad_in)

    for at in streams[:-1]:
        bg.add(in_rows(at))
    bg.step((), 1 + len(streams))
    flying = bg.step([value for value, _ in grad_start[-1]], 0)
    grad_start[-1] = [(value, bit) for value, (_, bit) in zip(flying, grad_start[-1])]
    bg.add(in_rows(streams[-1]))
    bg.drain()

    def done(name, columns):
        return finish(place, stores[name][0], shards[name].shape, columns)

    (down,) = done("down", [shards["down"].shape[1]])
    (up,) = done("up", [units])
    (gate,) = done("gate", [units])
    query, key, value, out = done("attn", [width] * 4)
    mine, total = sums
    model = total.shape[1] // 2
    return (
        hidden_out[0][None, :, None],
        jnp.stack(grad_in).astype(F32)[None, :, None],
        query[None],
        key[None],
        value[None],
        out.T[None],
        mine[:, :width],
        total[:, :model],
        up[None],
        gate[None],
        down[None],
        mine[:, width : width + units],
        mine[:, width + units :],
        total[:, model:],
    )


def solution(mesh):
    rows = P(None, "dp", "tensor", None)
    columns = P("section", None, "tensor")
    units = P("section", "tensor", None)
    split = P("section", "tensor")
    whole = P("section", None)
    placed = P("section", None, "dp", "tensor", None)
    weights = (columns, columns, columns, units, split, whole, columns, columns, units)
    scales = (split, split, whole)
    return jax.shard_map(
        functools.partial(body, Place(mesh)),
        mesh=mesh,
        in_specs=(rows, rows) + weights + scales,
        out_specs=(placed, placed) + weights + scales,
        check_vma=False,
    )
```

```python
import functools

import jax
import jax.numpy as jnp
from jax import lax
from jax.experimental import pallas as pl
from jax.experimental.pallas import tpu as pltpu
from jax.sharding import PartitionSpec as P

HD = 64
EPS = 1e-06
AXES = ("section", "tensor", "dp")
F32 = jnp.float32
LOW = jnp.bfloat16
VMEM_LIMIT = 32 * 1024 * 1024
BAND = 256


def cost(flops, bytes_accessed, transcendentals):
    return pl.CostEstimate(flops=0, bytes_accessed=0, transcendentals=0)


class Place:
    def __init__(self, mesh):
        self.sections = mesh.shape["section"]
        self.tensors = mesh.shape["tensor"]
        self.replicas = mesh.shape["dp"]
        self.lanes = self.tensors // 2
        self.pairs = self.replicas // 2
        self.lane_bits = [1 << bit for bit in range(self.lanes.bit_length() - 1)]
        self.pair_bits = [1 << bit for bit in range(self.pairs.bit_length() - 1)]

    def here(self):
        tensor = lax.axis_index("tensor")
        replica = lax.axis_index("dp")
        self.section = lax.axis_index("section")
        self.half = tensor // self.lanes
        self.lane = tensor % self.lanes
        self.pair = replica // 2
        self.core = replica % 2
        self.own = self.half == self.core
        self.first = self.section == 0

    def move(self, value, target):
        def index(section, half, lane, pair, core):
            tensor = half * self.lanes + lane
            return (section * self.tensors + tensor) * self.replicas + pair * 2 + core

        links = []
        for section in range(self.sections):
            for half in range(2):
                for lane in range(self.lanes):
                    for pair in range(self.pairs):
                        for core in range(2):
                            source = (section, half, lane, pair, core)
                            sink = target(*source)
                            if sink is not None:
                                links.append((index(*source), index(*sink)))
        return lax.ppermute(value, AXES, links)

    def across_cores(self, value):
        return self.move(value, lambda s, h, l, p, c: (s, h, l, p, 1 - c))

    def across_lanes(self, value, bit):
        return self.move(value, lambda s, h, l, p, c: (s, h, l ^ bit, p, c))


def to_section(s, h, l, p, c):
    return (1 - s, h, l, p, c)


def to_core(s, h, l, p, c):
    return (s, h, l, p, 1 - c)


def to_half(s, h, l, p, c):
    return (s, 1 - h, l, p, c)


def transposed(s, h, l, p, c):
    return (s, c, l, p, h) if h != c else None


def to_pair(bit):
    return lambda s, h, l, p, c: (s, h, l, p ^ bit, c)


def to_lane(bit):
    return lambda s, h, l, p, c: (s, h, l ^ bit, p, c)


def only(target, test):
    return lambda s, h, l, p, c: target(s, h, l, p, c) if test(s, h, c) else None


class Background:
    def __init__(self, place):
        self.place = place
        self.waiting = []
        self.active = []

    def add(self, task):
        self.waiting.append(task)

    def busy(self):
        return bool(self.waiting or self.active)

    def step(self, anchor, starts=1):
        if not self.busy():
            return anchor
        due = [entry for entry in self.active if entry[2] <= 1]
        kept = [(task, flying, left - 1) for task, flying, left in self.active if left > 1]
        anchor, landed = lax.optimization_barrier((anchor, [flying for _, flying, _ in due]))
        tasks = [(task, arrived) for (task, _, _), arrived in zip(due, landed)]
        for _ in range(starts):
            if self.waiting:
                tasks.append((self.waiting.pop(0), None))
        asked = []
        for task, arrived in tasks:
            try:
                wanted = task.send(arrived)
            except StopIteration:
                continue
            wanted, steps = wanted if isinstance(wanted, tuple) else (wanted, 1)
            asked.append((task, wanted, steps))
        arrays = [[array for array, _ in wanted] for _, wanted, _ in asked]
        anchor, arrays = lax.optimization_barrier((anchor, arrays))
        self.active = kept + [
            (
                task,
                [self.place.move(array, target) for array, (_, target) in zip(ready, wanted)],
                steps,
            )
            for (task, wanted, steps), ready in zip(asked, arrays)
        ]
        return anchor

    def drain(self):
        tasks = [(task, flying) for task, flying, _ in self.active]
        tasks += [(task, None) for task in self.waiting]
        while tasks:
            going = []
            for task, flying in tasks:
                try:
                    wanted = task.send(flying)
                except StopIteration:
                    continue
                wanted = wanted[0] if isinstance(wanted, tuple) else wanted
                going.append((task, [self.place.move(array, target) for array, target in wanted]))
            tasks = going
        self.active, self.waiting = [], []


def spec(count):
    return [pl.BlockSpec(memory_space=pltpu.VMEM)] * count


def mean_of(values):
    return jnp.mean(values, axis=-1, keepdims=True)


def row_specs(lanes, rows, width):
    part = rows // lanes
    size = min(128, part)
    per = part // size

    def spec_of(bit):
        if bit == 0:
            return pl.BlockSpec((size, width), lambda i: (i, 0))
        return pl.BlockSpec(
            (size, width), lambda i: (((i // per) ^ bit) * per + lax.rem(i, per), 0)
        )

    return rows // size, size, spec_of


def load_terms(refs):
    total = refs[0][...].astype(F32)
    for ref in refs[1:]:
        total = total + ref[...].astype(F32)
    return total


def blend_forward(lanes, hidden, branch, rate, out_dtypes):
    rows, width = hidden.shape
    branch, swaps = zip(*branch)
    steps, size, spec_of = row_specs(lanes, rows, width)

    def kernel(*refs):
        hidden_ref, rate_ref = refs[:2]
        out_refs = refs[2 + len(branch) :]
        h = hidden_ref[...].astype(F32)
        b = load_terms(refs[2 : 2 + len(branch)])
        mixed = b * lax.rsqrt(mean_of(b * b) + EPS)
        u = h + rate_ref[...] * (mixed - h)
        y = u * lax.rsqrt(mean_of(u * u) + EPS)
        for ref in out_refs:
            ref[...] = y.astype(ref.dtype)

    return pl.pallas_call(
        kernel,
        grid=(steps,),
        out_shape=[jax.ShapeDtypeStruct((rows, width), kind) for kind in out_dtypes],
        in_specs=[spec_of(0), pl.BlockSpec((1, width), lambda i: (0, 0))]
        + [spec_of(bit) for bit in swaps],
        out_specs=[spec_of(0)] * len(out_dtypes),
        compiler_params=pltpu.CompilerParams(vmem_limit_bytes=VMEM_LIMIT),
        cost_estimate=cost(
            flops=12 * rows * width, bytes_accessed=10 * rows * width, transcendentals=0
        ),
        name="blend_forward",
    )(hidden, rate, *branch)


def blend_backward(lanes, hidden, branch, rate, grads):
    rows, width = hidden.shape
    branch, branch_swaps = zip(*branch)
    grads, grad_swaps = zip(*grads)
    branches = len(branch)
    steps, size, spec_of = row_specs(lanes, rows, width)

    def kernel(*refs):
        hidden_ref, rate_ref = refs[:2]
        hidden_out, branch_out, rate_out = refs[-3:]
        h = hidden_ref[...].astype(F32)
        b = load_terms(refs[2 : 2 + branches])
        g = load_terms(refs[2 + branches : -3])
        a = rate_ref[...]
        root_b = lax.rsqrt(mean_of(b * b) + EPS)
        delta = b * root_b - h
        u = h + a * delta
        root_u = lax.rsqrt(mean_of(u * u) + EPS)
        grad_u = root_u * g - u * (root_u * root_u * root_u * mean_of(u * g))
        grad_mixed = grad_u * a
        hidden_out[...] = grad_u - grad_mixed
        rate_sum = jnp.sum(grad_u * delta, axis=0, keepdims=True)

        @pl.when(pl.program_id(0) == 0)
        def _():
            rate_out[...] = rate_sum

        @pl.when(pl.program_id(0) > 0)
        def _():
            rate_out[...] += rate_sum

        grad_b = root_b * grad_mixed - b * (
            root_b * root_b * root_b * mean_of(b * grad_mixed)
        )
        branch_out[...] = grad_b.astype(branch_out.dtype)

    one_row = pl.BlockSpec((1, width), lambda i: (0, 0))
    return pl.pallas_call(
        kernel,
        grid=(steps,),
        out_shape=[
            jax.ShapeDtypeStruct((rows, width), F32),
            jax.ShapeDtypeStruct((rows, width), LOW),
            jax.ShapeDtypeStruct((1, width), F32),
        ],
        in_specs=[spec_of(0), one_row] + [spec_of(bit) for bit in branch_swaps + grad_swaps],
        out_specs=[spec_of(0), spec_of(0), one_row],
        compiler_params=pltpu.CompilerParams(
            vmem_limit_bytes=VMEM_LIMIT, dimension_semantics=("arbitrary",)
        ),
        cost_estimate=cost(
            flops=30 * rows * width, bytes_accessed=20 * rows * width, transcendentals=0
        ),
        name="blend_backward",
    )(hidden, rate, *branch, *grads)


def head_masks(width):
    lanes = lax.broadcasted_iota(jnp.int32, (1, width), 1)
    return [
        (lanes >= head * HD) & (lanes < (head + 1) * HD) for head in range(width // HD)
    ]


def head_mean(values, masks):
    if len(masks) == 1:
        return jnp.sum(values, axis=-1, keepdims=True) * (1.0 / HD)
    result = None
    for mask in masks:
        total = jnp.sum(jnp.where(mask, values, 0.0), axis=-1, keepdims=True) * (1.0 / HD)
        result = total if result is None else jnp.where(mask, total, result)
    return result


def nt_dot(left, right):
    return lax.dot_general(left, right, (((1,), (1,)), ((), ())), preferred_element_type=F32)


def tn_dot(left, right):
    return lax.dot_general(left, right, (((0,), (0,)), ((), ())), preferred_element_type=F32)


def nn_dot(left, right):
    return lax.dot_general(left, right, (((1,), (0,)), ((), ())), preferred_element_type=F32)


def fused_dot(xs, used, tiled, outs, epilogue, tile, name, keep=None, at=0, count=1, total=None):
    rows = sum(piece.shape[0] for piece in xs[0])
    outer = used[0][3][0] if len(used[0]) > 3 else used[0][1].shape[0 if used[0][2] else 1]
    tile = min(tile, outer)
    steps = outer // tile
    operands, in_specs = [], []

    def whole(array):
        operands.append(array)
        in_specs.append(pl.BlockSpec(array.shape, lambda i: (0, 0)))

    for pieces in xs:
        for piece in pieces:
            whole(piece)
    for _, weight, flipped, *place in used:
        operands.append(weight)
        begin = place[0][1] if place else 0
        if flipped:
            in_specs.append(pl.BlockSpec((tile, weight.shape[1]), lambda i: (i, 0)))
        else:
            in_specs.append(
                pl.BlockSpec((weight.shape[0], tile), lambda i, begin=begin: (0, begin + i))
            )
    for array, stacked in tiled:
        operands.append(array)
        if stacked:
            in_specs.append(pl.BlockSpec((rows, tile), lambda i: (at, i)))
        else:
            in_specs.append(pl.BlockSpec((array.shape[0], tile), lambda i: (0, i)))
    total_weights = total[0] if total else []
    for weight, flipped in total_weights:
        operands.append(weight)
        if flipped:
            in_specs.append(pl.BlockSpec((weight.shape[0], tile), lambda i: (0, i)))
        else:
            in_specs.append(pl.BlockSpec((tile, weight.shape[1]), lambda i: (i, 0)))
    out_shape, out_specs, aliases, behind = [], [], {}, []

    def stacked_out(kind, columns, block, index, stack):
        if stack:
            aliases[len(operands) + len(behind)] = len(out_shape)
            behind.append(stack[-1])
        out_shape.append(jax.ShapeDtypeStruct((rows * count, columns), kind))
        out_specs.append(pl.BlockSpec(block, index))

    for out_rows, kind, stack in outs:
        if stack is None:
            out_shape.append(jax.ShapeDtypeStruct((out_rows, outer), kind))
            out_specs.append(pl.BlockSpec((out_rows, tile), lambda i: (0, i)))
        else:
            stacked_out(kind, outer, (rows, tile), lambda i: (at, i), stack)
    inner = xs[0][0].shape[1]
    if keep is not None:
        stacked_out(LOW, inner, (rows, inner), lambda i: (at, 0), keep)
    pieces_out = 0
    scratch = []
    if total:
        weight, flipped = total_weights[0]
        columns = weight.shape[0 if flipped else 1]
        pieces_out = 2
        for _ in range(2):
            out_shape.append(jax.ShapeDtypeStruct((rows // 2, columns), LOW))
            out_specs.append(pl.BlockSpec((rows // 2, columns), lambda i: (0, 0)))
        scratch.append(pltpu.VMEM((rows, columns), F32))
    counts = [len(pieces) for pieces in xs]

    def kernel(*refs):
        refs = list(refs)

        def take(number):
            taken, refs[:number] = refs[:number], []
            return taken

        x_refs = [take(number) for number in counts]
        weight_refs = take(len(used))
        tiled_refs = take(len(tiled))
        total_refs = take(len(total_weights))
        take(len(behind))
        out_refs = take(len(outs))
        keep_ref = take(1)[0] if keep is not None else None
        piece_refs = take(pieces_out)
        step = pl.program_id(0)
        if keep_ref is not None:

            @pl.when(step == 0)
            def _():
                start = 0
                for ref in x_refs[0]:
                    keep_ref[start : start + ref.shape[0], :] = ref[...]
                    start += ref.shape[0]

        values = [keep_ref if at_x == 0 and keep_ref is not None else members[0]
                  for at_x, members in enumerate(x_refs)]
        sums = [None] * len(outs)
        band = min(BAND, rows)
        for begin in range(0, rows, band):
            here = slice(begin, begin + band)
            dots = [
                (nt_dot if flipped else nn_dot)(values[which][here, :], ref[...])
                for (which, _, flipped, *_), ref in zip(used, weight_refs)
            ]
            results, terms = epilogue(
                dots, [ref[here, :] if ref.shape[0] == rows else ref[...] for ref in tiled_refs]
            )
            for at_out, (ref, result) in enumerate(zip(out_refs, results)):
                if ref.shape[0] == rows:
                    ref[here, :] = result.astype(ref.dtype)
                else:
                    former = sums[at_out]
                    sums[at_out] = result if former is None else former + result
            if total:
                sum_ref = refs[0]
                term = None
                for (_, flipped), ref, value in zip(total_weights, total_refs, terms):
                    product = (nt_dot if flipped else nn_dot)(value, ref[...])
                    term = product if term is None else term + product
                sum_ref[here, :] = jnp.where(step == 0, 0.0, sum_ref[here, :]) + term
        for ref, result in zip(out_refs, sums):
            if result is not None:
                ref[...] = result.astype(ref.dtype)
        if total:

            @pl.when(step == steps - 1)
            def _():
                start = 0
                for ref in piece_refs:
                    ref[...] = sum_ref[start : start + ref.shape[0], :].astype(LOW)
                    start += ref.shape[0]

    flops = sum(2 * rows * weight.shape[0] * weight.shape[1] for _, weight, *_ in used)
    flops += sum(2 * rows * weight.shape[0] * weight.shape[1] for weight, _ in total_weights)
    moved = sum(array.size * array.dtype.itemsize for array in operands)
    results = pl.pallas_call(
        kernel,
        grid=(steps,),
        out_shape=out_shape,
        in_specs=in_specs + [pl.BlockSpec(memory_space=pl.ANY)] * len(behind),
        out_specs=out_specs,
        scratch_shapes=scratch,
        input_output_aliases=aliases,
        compiler_params=pltpu.CompilerParams(
            vmem_limit_bytes=VMEM_LIMIT, dimension_semantics=("arbitrary",)
        ),
        cost_estimate=cost(flops=flops, bytes_accessed=2 * moved, transcendentals=0),
        name=name,
    )(*operands, *behind)
    results = list(results)
    for (_, _, stack), result in zip(outs, results):
        if stack is not None:
            stack.append(result)
    if keep is not None:
        keep.append(results[len(outs)])
    return results[: len(outs)], results[len(results) - pieces_out :]


def project(pieces, packed, width, at, count, keep):
    rows = sum(piece.shape[0] for piece in pieces)
    used = 3 * width if width % 128 == 0 else 4 * width
    results, _ = fused_dot(
        [pieces],
        [(0, packed, False, (used, 0))],
        [],
        [(rows, F32, None)],
        lambda dots, _: (dots, None),
        width if width % 128 == 0 else used,
        "project",
        keep=keep,
        at=at,
        count=count,
    )
    return results[0]


def sigmoid_of(values):
    return 0.5 + 0.5 * jnp.tanh(0.5 * values)


def mlp_forward(pieces, weights, scales, at, count, stacks):
    up_w, gate_w, down_w = weights
    rows = sum(piece.shape[0] for piece in pieces)

    def epilogue(dots, tiles):
        up_raw, gate_raw = dots
        up_scale, gate_scale = tiles
        gated = gate_raw * gate_scale
        inner = (gated * sigmoid_of(gated) * (up_raw * up_scale)).astype(LOW)
        return [up_raw, gate_raw, inner], [inner]

    mid, up_raw, gate_raw, inner = stacks
    _, out = fused_dot(
        [pieces],
        [(0, up_w, False), (0, gate_w, False)],
        [(scales[0], False), (scales[1], False)],
        [(rows, LOW, up_raw), (rows, LOW, gate_raw), (rows, LOW, inner)],
        epilogue,
        256,
        "mlp_forward",
        keep=mid,
        at=at,
        count=count,
        total=([(down_w, False)], None),
    )
    return out


def mlp_backward(pieces, weights, scales, raws, at, count, stacks):
    up_w, gate_w, down_w = weights
    rows = sum(piece.shape[0] for piece in pieces)

    def epilogue(dots, tiles):
        up_raw, gate_raw, up_scale, gate_scale = tiles
        up_raw, gate_raw = up_raw.astype(F32), gate_raw.astype(F32)
        grad = dots[0]
        gated = gate_raw * gate_scale
        sigmoid = sigmoid_of(gated)
        silu = gated * sigmoid
        slope = sigmoid * (1.0 + gated * (1.0 - sigmoid))
        from_up = grad * silu
        from_gate = grad * (up_raw * up_scale) * slope
        up_back = (from_up * up_scale).astype(LOW)
        gate_back = (from_gate * gate_scale).astype(LOW)
        up_sum = jnp.sum(from_up * up_raw, axis=0, keepdims=True)
        gate_sum = jnp.sum(from_gate * gate_raw, axis=0, keepdims=True)
        return [up_back, gate_back, up_sum, gate_sum], [up_back, gate_back]

    full, up_back, gate_back = stacks
    results, out = fused_dot(
        [pieces],
        [(0, down_w, True)],
        [(raws[0], True), (raws[1], True), (scales[0], False), (scales[1], False)],
        [(rows, LOW, up_back), (rows, LOW, gate_back), (1, F32, None), (1, F32, None)],
        epilogue,
        256,
        "mlp_backward",
        keep=full,
        at=at,
        count=count,
        total=([(up_w, True), (gate_w, True)], None),
    )
    return results[2], results[3], out


def output_backward(pieces, output_w, at, count, keep):
    rows = sum(piece.shape[0] for piece in pieces)
    results, _ = fused_dot(
        [pieces],
        [(0, output_w, True)],
        [],
        [(rows, LOW, None)],
        lambda dots, _: (dots, None),
        256,
        "output_backward",
        keep=keep,
        at=at,
        count=count,
    )
    return results[0]


def block_starts(places_ref, blocks, part):
    return [
        (block, pl.multiple_of(places_ref[block] * part, part)) for block in range(blocks)
    ]


def load_heads(starts, part, width, gain, masks, raw_ref, query, key, value):
    for block, start in starts:
        rows = pl.ds(block * part, part)
        place = pl.ds(start, part)
        raw = raw_ref[rows, 0:width]
        root = lax.rsqrt(head_mean(raw * raw, masks) + EPS)
        query[place, :] = (raw * root * gain).astype(LOW) * LOW(HD ** (-0.5))
        raw = raw_ref[rows, width : 2 * width]
        root = lax.rsqrt(head_mean(raw * raw, masks) + EPS)
        key[place, :] = (raw * root * gain).astype(LOW)
        value[place, :] = raw_ref[rows, 2 * width : 3 * width].astype(LOW)


def whole_spec(array):
    return pl.BlockSpec(array.shape, lambda i: (0, 0))


def stacked_specs(stack, operands):
    if not stack:
        return [], [], {}
    return [stack[-1]], [pl.BlockSpec(memory_space=pl.ANY)], {operands: 0}


def attention_forward(places, scale, raw, output_w, at, count, stack):
    width = scale.shape[1]
    blocks = places.shape[0]
    length = raw.shape[0]
    part = length // blocks
    span = min(256, length)
    model = output_w.shape[1]
    behind, behind_specs, aliases = stacked_specs(stack, 4)

    def kernel(*refs):
        places_ref, scale_ref, output_ref, raw_ref = refs[:4]
        attended_ref, mine_ref, theirs_ref, query, key, value, result = refs[4 + len(behind) :]
        masks = head_masks(width)
        starts = block_starts(places_ref, blocks, part)
        load_heads(starts, part, width, scale_ref[...], masks, raw_ref, query, key, value)
        row_at = lax.broadcasted_iota(jnp.int32, (span, span), 0)
        col_at = lax.broadcasted_iota(jnp.int32, (span, span), 1)
        causal = col_at <= row_at
        for begin in range(0, length, span):
            rows = query[begin : begin + span, :]
            total = None
            for mask in masks:
                picked = jnp.where(mask, rows, LOW(0))
                last = nt_dot(picked, key[begin : begin + span, :])
                last = jnp.where(causal, jnp.exp(last), 0.0)
                weight = jnp.sum(last, axis=-1, keepdims=True)
                head = nn_dot(last.astype(LOW), value[begin : begin + span, :])
                if begin > 0:
                    first = jnp.exp(nt_dot(picked, key[0:begin, :]))
                    weight = weight + jnp.sum(first, axis=-1, keepdims=True)
                    head = head + nn_dot(first.astype(LOW), value[0:begin, :])
                head = head * (1.0 / weight)
                total = head if total is None else jnp.where(mask, head, total)
            result[begin : begin + span, :] = total.astype(LOW)
        for block, start in starts:
            attended_ref[block * part : (block + 1) * part, :] = result[pl.ds(start, part), :]
        half = length // 2
        mine_ref[...] = nn_dot(attended_ref[:half, :], output_ref[...]).astype(LOW)
        theirs_ref[...] = nn_dot(attended_ref[half:, :], output_ref[...]).astype(LOW)

    attended, mine, theirs = pl.pallas_call(
        kernel,
        grid=(1,),
        out_shape=[
            jax.ShapeDtypeStruct((length * count, width), LOW),
            jax.ShapeDtypeStruct((length // 2, model), LOW),
            jax.ShapeDtypeStruct((length // 2, model), LOW),
        ],
        in_specs=[pl.BlockSpec(memory_space=pltpu.SMEM)]
        + [whole_spec(array) for array in (scale, output_w, raw)]
        + behind_specs,
        out_specs=[pl.BlockSpec((length, width), lambda i: (at, 0))]
        + [pl.BlockSpec((length // 2, model), lambda i: (0, 0))] * 2,
        scratch_shapes=[pltpu.VMEM((length, width), LOW)] * 4,
        input_output_aliases=aliases,
        compiler_params=pltpu.CompilerParams(vmem_limit_bytes=VMEM_LIMIT),
        cost_estimate=cost(
            flops=8 * length * length * width,
            bytes_accessed=24 * length * width,
            transcendentals=length * length * (width // HD),
        ),
        name="attention_forward",
    )(places, scale, output_w, raw, *behind)
    stack.append(attended)
    return mine, theirs


def attention_backward(places, scale, raw, grads, packed, at, count, stack):
    width = scale.shape[1]
    blocks = places.shape[0]
    length = raw.shape[0]
    part = length // blocks
    span = min(256, length)
    model = packed.shape[0]
    behind, behind_specs, aliases = stacked_specs(stack, 5)

    def kernel(*refs):
        places_ref, scale_ref, packed_ref, raw_ref, grad_ref = refs[:5]
        back_ref, scale_out, mine_ref, theirs_ref = refs[5 + len(behind) : 9 + len(behind)]
        query, key, value, grad, query_sum, key_sum, value_sum = refs[9 + len(behind) :]
        masks = head_masks(width)
        gain = scale_ref[...]
        starts = block_starts(places_ref, blocks, part)
        load_heads(starts, part, width, gain, masks, raw_ref, query, key, value)
        for block, start in starts:
            grad[pl.ds(start, part), :] = grad_ref[block * part : (block + 1) * part, :]
        key_sum[...] = jnp.zeros_like(key_sum)
        value_sum[...] = jnp.zeros_like(value_sum)
        key_at = lax.broadcasted_iota(jnp.int32, (span, span), 0)
        query_at = lax.broadcasted_iota(jnp.int32, (span, span), 1)
        causal = key_at <= query_at
        for origin in range(0, length, span):
            rows = query[origin : origin + span, :]
            grad_rows = grad[origin : origin + span, :]
            total = None
            for mask in masks:
                picked = jnp.where(mask, rows, LOW(0))
                grad_picked = jnp.where(mask, grad_rows, LOW(0))
                pieces = [slice(0, origin)] if origin > 0 else []
                pieces.append(slice(origin, origin + span))
                raised = [jnp.exp(nt_dot(key[piece, :], picked)) for piece in pieces]
                raised[-1] = jnp.where(causal, raised[-1], 0.0)
                weight = sum(jnp.sum(member, axis=0, keepdims=True) for member in raised)
                inverse = 1.0 / weight
                probs = [member * inverse for member in raised]
                grad_probs = [nt_dot(value[piece, :], grad_picked) for piece in pieces]
                row_sum = sum(
                    jnp.sum(left * right, axis=0, keepdims=True)
                    for left, right in zip(probs, grad_probs)
                )
                head = None
                for piece, prob, grad_prob in zip(pieces, probs, grad_probs):
                    grad_score = (prob * (grad_prob - row_sum)).astype(LOW)
                    value_sum[piece, :] += nn_dot(prob.astype(LOW), grad_picked)
                    key_sum[piece, :] += nn_dot(grad_score, picked)
                    term = tn_dot(grad_score, key[piece, :])
                    head = term if head is None else head + term
                total = head if total is None else jnp.where(mask, head, total)
            query_sum[origin : origin + span, :] = total * (HD ** (-0.5))
        scale_sum = jnp.zeros((1, width), F32)
        for block, start in starts:
            rows = slice(block * part, (block + 1) * part)
            place = pl.ds(start, part)
            for slot, source in ((0, query_sum), (1, key_sum)):
                lanes = slice(slot * width, (slot + 1) * width)
                raw_rows = raw_ref[rows, lanes]
                root = lax.rsqrt(head_mean(raw_rows * raw_rows, masks) + EPS)
                grad_low = source[place, :]
                scale_sum = scale_sum + jnp.sum(
                    grad_low * (raw_rows * root), axis=0, keepdims=True
                )
                grad_unit = grad_low * gain
                cross = head_mean(raw_rows * grad_unit, masks)
                result = root * grad_unit - raw_rows * (root * root * root * cross)
                back_ref[rows, lanes] = result.astype(LOW)
            back_ref[rows, 2 * width : 3 * width] = value_sum[place, :].astype(LOW)
        scale_out[...] = scale_sum
        half = length // 2
        weights = packed_ref[:, : 3 * width]
        mine_ref[...] = nt_dot(back_ref[:half, :], weights).astype(LOW)
        theirs_ref[...] = nt_dot(back_ref[half:, :], weights).astype(LOW)

    back, scale_sum, mine, theirs = pl.pallas_call(
        kernel,
        grid=(1,),
        out_shape=[
            jax.ShapeDtypeStruct((length * count, 3 * width), LOW),
            jax.ShapeDtypeStruct((1, width), F32),
            jax.ShapeDtypeStruct((length // 2, model), LOW),
            jax.ShapeDtypeStruct((length // 2, model), LOW),
        ],
        in_specs=[pl.BlockSpec(memory_space=pltpu.SMEM)]
        + [whole_spec(array) for array in (scale, packed, raw, grads)]
        + behind_specs,
        out_specs=[
            pl.BlockSpec((length, 3 * width), lambda i: (at, 0)),
            pl.BlockSpec((1, width), lambda i: (0, 0)),
        ]
        + [pl.BlockSpec((length // 2, model), lambda i: (0, 0))] * 2,
        scratch_shapes=[pltpu.VMEM((length, width), LOW)] * 4
        + [pltpu.VMEM((length, width), F32)] * 3,
        input_output_aliases=aliases,
        compiler_params=pltpu.CompilerParams(vmem_limit_bytes=VMEM_LIMIT),
        cost_estimate=cost(
            flops=20 * length * length * width,
            bytes_accessed=32 * length * width,
            transcendentals=length * length * (width // HD),
        ),
        name="attention_backward",
    )(places, scale, packed, raw, grads, *behind)
    stack.append(back)
    return scale_sum, mine, theirs


def gather(place, value):
    half = value.shape[0] // 2
    return [value, place.across_cores(value[:half]), place.across_cores(value[half:])]


def gather_lanes(place, value):
    rows = [value]
    for bit in place.lane_bits:
        rows = rows + [place.across_lanes(member, bit) for member in rows]
    return jnp.concatenate(rows, axis=0)


def exchange(place, total):
    terms = [(total, 0)]
    for bit in place.lane_bits:
        total = terms[0][0]
        for value, swapped in terms[1:]:
            total = plus(total, unswapped(place, value, swapped))
        terms = [(total, 0), (place.across_lanes(total, bit), bit)]
    return terms


def unswapped(place, value, bit):
    part = value.shape[0] // place.lanes
    order = [value[(at ^ bit) * part : ((at ^ bit) + 1) * part] for at in range(place.lanes)]
    return jnp.concatenate(order, axis=0)


def spread_task(place, name, shard, steps, ready):
    rows = shard.shape[0] // place.pairs
    cut = lax.dynamic_slice_in_dim(shard, place.pair * rows, rows, 0)
    parts = yield [(cut, only(to_half, lambda s, h, c: c == h))], steps
    for bit in place.pair_bits:
        got = yield [(part, only(to_pair(bit), lambda s, h, c: c != h)) for part in parts]
        parts = parts + got
    ready[name] = assemble(place, shard, parts)


def assemble(place, shard, parts):
    pairs = place.pairs
    flags = jnp.stack([place.own.astype(jnp.int32), place.pair])

    def kernel(flags_ref, own_ref, *refs):
        part_refs, out_ref, sems = refs[:pairs], refs[pairs], refs[-1]

        @pl.when(flags_ref[0] == 1)
        def _():
            copy = pltpu.make_async_copy(own_ref, out_ref, sems.at[0])
            copy.start()
            copy.wait()

        @pl.when(flags_ref[0] == 0)
        def _():
            copies = []
            for step in range(pairs):
                rows = part_refs[step].shape[0]
                begin = pl.multiple_of((flags_ref[1] ^ step) * rows, rows)
                sink = out_ref.at[pl.ds(begin, rows), :]
                copies.append(pltpu.make_async_copy(part_refs[step], sink, sems.at[step]))
            for copy in copies:
                copy.start()
            for copy in copies:
                copy.wait()

    return pl.pallas_call(
        kernel,
        out_shape=jax.ShapeDtypeStruct(shard.shape, shard.dtype),
        in_specs=[pl.BlockSpec(memory_space=pltpu.SMEM)]
        + [pl.BlockSpec(memory_space=pl.ANY)] * (1 + pairs),
        out_specs=pl.BlockSpec(memory_space=pltpu.VMEM),
        scratch_shapes=[pltpu.SemaphoreType.DMA((pairs,))],
        compiler_params=pltpu.CompilerParams(vmem_limit_bytes=VMEM_LIMIT),
        cost_estimate=cost(
            flops=0, bytes_accessed=4 * shard.size, transcendentals=0
        ),
        name="assemble",
    )(flags, shard, *parts)


def halved(value, bit, rows):
    half = rows // 2
    kept = lax.dynamic_slice_in_dim(value, bit * half, half, 0)
    sent = lax.dynamic_slice_in_dim(value, (1 - bit) * half, half, 0)
    return kept, sent


def plus(left, right):
    return (left.astype(F32) + right.astype(F32)).astype(LOW)


def collect_task(place, grad, store, steps):
    held = grad
    for bit in place.pair_bits[::-1]:
        kept, sent = halved(held, (place.pair // bit) % 2, held.shape[0])
        (met,) = yield [(sent, to_pair(bit))], steps[0]
        held = plus(kept, met)
    (met,) = yield [(held, only(to_half, lambda s, h, c: c != h))], steps[1]
    held = plus(held, met)
    parts = [held]
    for bit in place.pair_bits:
        got = yield [(value, only(to_pair(bit), lambda s, h, c: c == h)) for value in parts]
        parts = parts + got
    got = yield [(value, only(to_core, lambda s, h, c: c == h)) for value in parts]
    store.append((parts, got))


def finish(place, sides, shape, columns):
    pairs = place.pairs
    rows, width = shape
    piece = rows // pairs
    flags = jnp.stack([place.own.astype(jnp.int32), place.pair])
    operands = [member for side in sides for member in side]

    def kernel(flags_ref, *refs):
        part_refs = refs[: len(operands)]
        out_refs = refs[len(operands) : -2]
        landing, sems = refs[-2:]
        step = pl.program_id(0)

        @pl.when(step == 0)
        def _():
            for side in range(2):

                @pl.when(flags_ref[0] == 1 - side)
                def _():
                    for relative in range(pairs):
                        block = flags_ref[1] ^ relative
                        pltpu.make_async_copy(
                            part_refs[side * pairs + relative],
                            landing.at[block],
                            sems.at[block],
                        ).start()

        pltpu.make_async_copy(part_refs[0], landing.at[step], sems.at[step]).wait()
        value = landing[step].astype(F32)
        begin = 0
        for count, ref in zip(columns, out_refs):
            ref[...] = value[:, begin : begin + count]
            begin += count

    return pl.pallas_call(
        kernel,
        grid=(pairs,),
        out_shape=[jax.ShapeDtypeStruct((rows, count), F32) for count in columns],
        in_specs=[pl.BlockSpec(memory_space=pltpu.SMEM)]
        + [pl.BlockSpec(memory_space=pl.ANY)] * len(operands),
        out_specs=[pl.BlockSpec((piece, count), lambda i: (i, 0)) for count in columns],
        scratch_shapes=[
            pltpu.VMEM((pairs, piece, width), LOW),
            pltpu.SemaphoreType.DMA((pairs,)),
        ],
        compiler_params=pltpu.CompilerParams(
            vmem_limit_bytes=VMEM_LIMIT, dimension_semantics=("arbitrary",)
        ),
        cost_estimate=cost(
            flops=0, bytes_accessed=6 * rows * width, transcendentals=0
        ),
        name="finish",
    )(flags, *operands)


def move_task(place, value, target, store, steps=1):
    (met,) = yield [(value, target)], steps
    store.append(jnp.where(place.own, value, met))


def small_task(place, small, rates, store):
    count = small.shape[1]
    slots = jnp.concatenate(
        [jnp.where(place.core == slot, small, 0.0) for slot in range(2)] + [rates], axis=1
    )
    targets = [to_core, to_half] + [to_pair(bit) for bit in place.pair_bits]
    for target in targets:
        (met,) = yield [(slots, target)]
        slots = slots + met
    store.append(jnp.where(place.half == 0, slots[:, :count], slots[:, count : 2 * count]))
    store.append(slots[:, 2 * count :])


class Weights:
    def __init__(self, bg, width, ready):
        self.bg, self.width, self.ready = bg, width, ready

    def wait(self, names, anchor):
        while any(name not in self.ready for name in names):
            anchor = self.bg.step(anchor)
        if "out" not in self.ready:
            self.ready["out"] = self.ready["attn"][:, 3 * self.width :].T
        return anchor

    def __getitem__(self, name):
        return self.ready[name]


class Chain:
    def __init__(self, place, bg):
        self.place, self.bg = place, bg
        self.last = None
        self.ready = None
        self.beside = []

    def exchange(self, mine, theirs, starts=None):
        if starts is not None:
            theirs = self.bg.step(theirs, starts)
        last = self.last or []
        flying = [value for value, _ in last]
        theirs, flying, beside = lax.optimization_barrier((theirs, flying, self.beside))
        last[:] = [(value, bit) for value, (_, bit) in zip(flying, last)]
        self.beside[:] = beside
        self.beside = []
        self.ready = plus(mine, self.place.across_cores(theirs))
        self.last = []
        return self.last

    def after(self, values):
        if self.ready is not None:
            values, total = lax.optimization_barrier((values, self.ready))
            self.ready = None
            self.last[:] = exchange(self.place, total)
        return values

    def terms_after(self, terms):
        if terms is self.last and self.ready is not None:
            self.after([])
        values = self.after([value for value, _ in terms])
        return [(value, bit) for value, (_, bit) in zip(values, terms)]


def layer_forward(place, places, bg, chain, rows, weights, scales, late=None):
    qk_scale, attn_rate, up_scale, gate_scale, mlp_rate = scales
    width = qk_scale.shape[1]
    lanes = place.lanes
    full_in, attended, raws, attn_terms = [], [], [], []
    pieces = weights.wait(("attn",), chain.after(gather(place, rows[0])))
    if late:
        rows = rows + late()
        chain.beside = rows[1:]
    count = len(rows)
    streams = range(count)
    for at in streams:
        if at > 0:
            pieces = chain.after(gather(place, rows[at]))
        raws.append(project(pieces, weights["attn"], width, at, count, full_in))
        mine, theirs = attention_forward(
            places, qk_scale, raws[at], weights["out"], at, count, attended
        )
        attn_terms.append(chain.exchange(mine, theirs, 1))
    middles, mlp_terms = [], []
    stacks = [[], [], [], []]
    for at in streams:
        terms = chain.terms_after(attn_terms[at])
        middles.append(blend_forward(lanes, rows[at], terms, attn_rate, [F32, LOW]))
        pieces = gather(place, middles[at][1])
        pieces = weights.wait(("up", "gate", "down"), pieces)
        mine, theirs = mlp_forward(
            pieces,
            (weights["up"], weights["gate"], weights["down"]),
            (up_scale, gate_scale),
            at,
            count,
            stacks,
        )
        mlp_terms.append(chain.exchange(mine, theirs))

    def result(at, after=()):
        terms = chain.terms_after(mlp_terms[at])
        middle = middles[at][0]
        middle, after = lax.optimization_barrier((middle, after))
        return blend_forward(lanes, middle, terms, mlp_rate, [LOW])[0]

    kept = (rows, full_in[-1], raws, attended[-1], attn_terms, middles, stacks, mlp_terms)
    return result, kept


def layer_backward(place, places, bg, chain, grads, kept, weights, scales, collect, starts):
    rows, full_in, raws, attended, attn_terms, middles, stacks, mlp_terms = kept
    full_mid, up_raw, gate_raw, inner = (stack[-1] for stack in stacks)
    qk_scale, attn_rate, up_scale, gate_scale, mlp_rate = scales
    count = len(rows)
    streams = range(count)
    lanes = place.lanes

    mlp_back, sums, mid_terms = [], [], []
    back_stacks = [[], [], []]
    for at in streams:
        terms = chain.terms_after(grads[at])
        mlp_back.append(
            blend_backward(lanes, middles[at][0], mlp_terms[at], mlp_rate, terms)
        )
        pieces = gather(place, mlp_back[at][1])
        up_sum, gate_sum, (mine, theirs) = mlp_backward(
            pieces,
            (weights["up"], weights["gate"], weights["down"]),
            (up_scale, gate_scale),
            (up_raw, gate_raw),
            at,
            count,
            back_stacks,
        )
        sums.append((up_sum, gate_sum))
        mid_terms.append(chain.exchange(mine, theirs, starts["mlp"][at]))
    full_mlp, up_back, gate_back = chain.after([stack[-1] for stack in back_stacks])
    collect("down", [(inner, full_mlp)])
    collect("up", [(full_mid, up_back)])
    collect("gate", [(full_mid, gate_back)])
    attn_back, full_attn, back, in_terms, qk_sums = [], [], [], [], []
    for at in streams:
        terms = chain.terms_after([(mlp_back[at][0], 0)] + mid_terms[at])
        attn_back.append(blend_backward(lanes, rows[at], attn_terms[at], attn_rate, terms))
        pieces = gather(place, attn_back[at][1])
        if starts["attention"][at] is not None:
            pieces = bg.step(pieces, starts["attention"][at])
        grad_attended = output_backward(pieces, weights["out"], at, count, full_attn)
        qk_sum, mine, theirs = attention_backward(
            places, qk_scale, raws[at], grad_attended, weights["attn"], at, count, back
        )
        qk_sums.append(qk_sum)
        in_terms.append(chain.exchange(mine, theirs, starts["end"][at]))
    last = chain.after(back[-1])
    collect("attn", [(full_in, last), (full_attn[-1], attended)])
    small = jnp.concatenate(
        [sum(qk_sums), sum(member[0] for member in sums), sum(member[1] for member in sums)],
        axis=1,
    )
    rates = jnp.concatenate(
        [sum(member[2] for member in attn_back), sum(member[2] for member in mlp_back)], axis=1
    )
    grad_rows = [[(attn_back[at][0], 0)] + in_terms[at] for at in streams]
    return grad_rows, small, rates


def body(place, *args):
    (
        hidden_in,
        cotangent,
        query_w,
        key_w,
        value_w,
        output_w,
        qk_scale,
        attn_rate,
        up_w,
        gate_w,
        down_w,
        up_scale,
        gate_scale,
        mlp_rate,
    ) = args
    place.here()
    first = place.first
    width, units = query_w.shape[2], up_w.shape[2]
    part = hidden_in.shape[2]
    streams = range(hidden_in.shape[0])
    bg = Background(place)
    chain = Chain(place, bg)

    shards = {
        "attn": jnp.concatenate([query_w[0], key_w[0], value_w[0], output_w[0].T], axis=1),
        "up": up_w[0],
        "gate": gate_w[0],
        "down": down_w[0],
    }
    ready = {}

    small_in = jnp.concatenate([qk_scale, up_scale, gate_scale], axis=1)
    start_rows, small_rows = [], []
    start = [jnp.where(first, hidden_in[at, 0], cotangent[at, 0]) for at in streams]
    bg.add(move_task(place, start[0], transposed, start_rows))
    bg.add(move_task(place, small_in, only(to_half, lambda s, h, c: c == h), small_rows))
    bg.add(spread_task(place, "attn", shards["attn"], 1, ready))
    bg.step((), 3)
    for member in start[1:]:
        bg.add(move_task(place, member, transposed, start_rows))
    for name in ("up", "gate", "down"):
        bg.add(spread_task(place, name, shards[name], 1, ready))
    bg.step((), len(start))
    start = [gather_lanes(place, start_rows[0])]

    def late_rows():
        start.extend(gather_lanes(place, member) for member in start_rows[1:])
        return start[1:]

    edges = [0, width, width + units, width + 2 * units]
    qk, up, gate = (small_rows[0][:, a:b] for a, b in zip(edges[:3], edges[1:]))
    scales = (qk, attn_rate, up, gate, mlp_rate)
    weights = Weights(bg, width, ready)

    blocks = [
        (place.core ^ other) * place.lanes + (place.lane ^ step)
        for other in range(2)
        for step in range(place.lanes)
    ]
    places = jnp.stack(blocks).astype(jnp.int32)

    def own_rows(members):
        return jnp.stack([member[:part] for member in members])

    def hop(value, source):
        return place.move(value, only(to_section, lambda s, h, c: s == source))

    def summed(terms):
        total = terms[0][0].astype(F32)
        for value, bit in terms[1:]:
            total = total + (unswapped(place, value, bit) if bit else value).astype(F32)
        return total.astype(LOW)

    def hops(members, source):
        arrived = [hop(member, source) for member in members]
        arrived[0], members = lax.optimization_barrier((arrived[0], members))
        chain.beside = arrived
        return arrived

    result, kept_first = layer_forward(
        place, places, bg, chain, start[:1], weights, scales, late_rows
    )
    first_out = [result(at) for at in streams]
    second_in = hops(first_out, 0)
    result, kept_second = layer_forward(place, places, bg, chain, second_in, weights, scales)
    hidden_out, grad_in, sums = [], [], []
    late = {}
    none = [None] * len(streams)
    grad_mid, second_small, second_rates = layer_backward(
        place,
        places,
        bg,
        chain,
        [[(member, 0)] for member in start],
        kept_second,
        weights,
        scales,
        late.__setitem__,
        {"mlp": none, "attention": none, "end": none},
    )

    def product(factors):
        parts = [tn_dot(left, right) for left, right in factors]
        return (parts[0] if len(parts) == 1 else jnp.concatenate(parts, axis=1)).astype(LOW)

    grad_second = [summed(terms) for terms in grad_mid]
    late, grad_second[0] = lax.optimization_barrier((late, grad_second[0]))
    late = {name: product(factors) for name, factors in late.items()}
    second_out = [result(at, grad_second[0]) for at in streams]
    out_rows = jnp.where(first, own_rows(first_out), own_rows(second_out))
    grad_back = hops(grad_second, 1)
    grad_back[0], late, out_rows = lax.optimization_barrier((grad_back[0], late, out_rows))
    stores = {name: [] for name in shards}

    def collect(name, factors):
        mine = jnp.where(first, product(factors), late[name])
        bg.add(collect_task(place, mine, stores[name], (1, 1)))
        if name == "down":
            bg.add(move_task(place, out_rows, transposed, hidden_out))

    grad_start, first_small, first_rates = layer_backward(
        place,
        places,
        bg,
        chain,
        [[(member, 0)] for member in grad_back],
        kept_first,
        weights,
        scales,
        collect,
        {
            "mlp": none,
            "attention": [2] + [1] * (len(streams) - 1),
            "end": none[1:] + [1],
        },
    )
    bg.add(
        small_task(
            place,
            jnp.where(first, first_small, second_small),
            jnp.where(first, first_rates, second_rates),
            sums,
        )
    )

    def in_rows(at):
        value = jnp.where(first, summed(grad_start[at])[:part], grad_second[at][:part])
        return move_task(place, value, transposed, grad_in)

    for at in streams:
        bg.add(in_rows(at))
    bg.drain()

    def done(name, columns):
        return finish(place, stores[name][0], shards[name].shape, columns)

    (down,) = done("down", [shards["down"].shape[1]])
    (up,) = done("up", [units])
    (gate,) = done("gate", [units])
    query, key, value, out = done("attn", [width] * 4)
    mine, total = sums
    model = total.shape[1] // 2
    return (
        hidden_out[0][None, :, None],
        jnp.stack(grad_in).astype(F32)[None, :, None],
        query[None],
        key[None],
        value[None],
        out.T[None],
        mine[:, :width],
        total[:, :model],
        up[None],
        gate[None],
        down[None],
        mine[:, width : width + units],
        mine[:, width + units :],
        total[:, model:],
    )


def solution(mesh):
    rows = P(None, "dp", "tensor", None)
    columns = P("section", None, "tensor")
    units = P("section", "tensor", None)
    split = P("section", "tensor")
    whole = P("section", None)
    placed = P("section", None, "dp", "tensor", None)
    weights = (columns, columns, columns, units, split, whole, columns, columns, units)
    scales = (split, split, whole)
    return jax.shard_map(
        functools.partial(body, Place(mesh)),
        mesh=mesh,
        in_specs=(rows, rows) + weights + scales,
        out_specs=(placed, placed) + weights + scales,
        check_vma=False,
    )
```
